512 devices in a mesh: seq: 64 (over z, y), tp: 8 (over x, core).
Axes of the slice: x: 4, y: 4, z: 16, core: 2. Of those that a mesh axis runs over, the one named last changes fastest.
Arguments:
- queries: bfloat16 [64, 64, 128], P('seq', 'tp'), may hold values from -160 to 160
- key_codes: bfloat16 [524288, 8, 128], P('seq', 'tp'), may hold values from -127 to 127, as said below
- key_scale: float32 [4096, 8, 128], P('seq', 'tp'), may hold values from 0.005 to 0.03
- outlier_chan: int32 [4096, 8, 8], P('seq', 'tp'), may hold values from 0 to 127
- outlier_val: bfloat16 [524288, 8, 8], P('seq', 'tp'), may hold values from -12 to 12
- value_codes: bfloat16 [524288, 8, 128], P('seq', 'tp'), may hold values from -127 to 127, as said below
- value_scale: float32 [4096, 8, 128], P('seq', 'tp'), may hold values from 0.005 to 0.03
- suffix_keys: bfloat16 [256, 128, 8, 128], P('seq', None, 'tp'), may hold values from -10 to 10
- suffix_values: bfloat16 [256, 128, 8, 128], P('seq', None, 'tp'), may hold values from -6 to 6
- page_table: int32 [64, 4], P('seq'), may hold values from 0 to 3, as said below
- suffix_len: int32 [64], P('seq'), may hold values from 1 to 512, as said below
- out_weight: bfloat16 [8192, 8192], P('tp', 'seq'), may hold values from -0.5 to 0.5
Outputs:
- output: bfloat16 [64, 8192], P('tp', 'seq')
The draws below stay inside these ranges and needn't reach their ends.
Inputs may be any that keep to these rules, and one draw needn't show every extreme that they name: `key_codes`: whole numbers. `value_codes`: whole numbers. `page_table`: the 1 samples b with the same b // 1 name each of the 4 pages of their pool exactly once. `suffix_len`: some sample has all 512 positions live.
All inputs are finite; a program needn't handle non-finite values.
Results may differ from the reference program's by a relative error of at most 0.018.
The reference program's roundings to bfloat16 on the way count: a program that leaves them out, or rounds other values in their place, can miss the bound.
Values may be sent and summed in bfloat16 or wider, within the bound.
No kernel may reach another device: no remote copies, remote signals or barrier semaphores. Data moves between devices by JAX's collectives and lax.ppermute only.
A program may use at most 64 MiB of HBM per device.

```python
import math
import jax
import jax.numpy as jnp
from jax import lax

D = 8192
QH = 64
KVH = 8
HD = 128
PAGE = 128
OUT = 8
SPAGE = 128
SP_PER = 4
B_DEV = 1
QPK = 8
B = 64
PREFIX = 524288
POOL = 4
POOLS = 256
S_MAX = 512


def draw_queries(key, part):
    key = jax.random.fold_in(key, 11)
    draw_one = jax.random.fold_in(key, 0)
    base = jnp.clip(jax.random.normal(draw_one, (B, QH, HD), jnp.float32), -4.0, 4.0)
    return (2.0 * base).astype(jnp.bfloat16)


def draw_key_codes(key, part):
    key = jax.random.fold_in(key, 21)
    return jax.random.randint(key, (PREFIX, KVH, HD), -127, 128).astype(jnp.float32).astype(jnp.bfloat16)


def draw_value_codes(key, part):
    key = jax.random.fold_in(key, 22)
    return jax.random.randint(key, (PREFIX, KVH, HD), -127, 128).astype(jnp.float32).astype(jnp.bfloat16)


def draw_page_table(key, part):
    key = jax.random.fold_in(key, 31)
    device_keys = jax.random.split(key, B // B_DEV)
    orders = jax.vmap(lambda single: jax.random.permutation(single, POOL))(device_keys)
    return orders.reshape(B, SP_PER).astype(jnp.int32)


def draw_suffix_len(key, part):
    key = jax.random.fold_in(key, 41)
    draw_one, draw_two = jax.random.split(key)
    lengths = jax.random.randint(draw_one, (B,), 1, S_MAX + 1)
    chosen = jax.random.randint(draw_two, (), 0, B)
    return lengths.at[chosen].set(S_MAX).astype(jnp.int32)


def set_ends(drawn, stream_key, low, top_value):
    dims = drawn.shape
    place = [jax.random.randint(jax.random.fold_in(stream_key, axis), (), 0, dims[axis]) for axis in range(len(dims))]
    drawn = drawn.at[tuple(place)].set(low)
    longest = dims.index(max(dims))
    place[longest] = (place[longest] + 1) % dims[longest]
    return drawn.at[tuple(place)].set(top_value)


def steps_of(own_key, extent, shards, smallest, largest):
    def one(axis_at, blocks):
        draws = jax.random.uniform(jax.random.fold_in(jax.random.fold_in(own_key, 6), axis_at), (blocks,), jnp.float32, smallest / len(shards), largest / len(shards))
        return jnp.repeat(jnp.exp(draws), extent[axis_at] // blocks).reshape((-1,) + (1,) * (len(extent) - axis_at - 1))

    loudness = one(*shards[0])
    for cut in shards[1:]:
        loudness = loudness * one(*cut)
    return loudness


def scatter_about(rng, shape, deviation, most, pieces=(), held_as=jnp.bfloat16):
    values = deviation * jax.random.normal(rng, shape, jnp.float32)
    if pieces:
        values = values * steps_of(rng, shape, pieces, -0.22, 0.18)
    return jnp.clip(values, -most, most).astype(held_as)


def setup_inputs(seed: int = 0) -> dict:
    streams_of = jax.random.split(jax.random.key(seed), 13)
    queries = draw_queries(jax.random.fold_in(streams_of[12], 71), 0)
    key_codes = draw_key_codes(jax.random.fold_in(streams_of[12], 71), 0)
    key_scale = jnp.clip(jnp.exp(math.log(0.03) - 1.7917595 * jax.random.uniform(streams_of[2], (PREFIX // PAGE, KVH, HD), jnp.float32) ** steps_of(streams_of[2], (PREFIX // PAGE, KVH, HD), ((0, 64), (1, 8)), -0.2, 0.2)), 0.005, 0.03)
    outlier_chan = set_ends(jax.random.randint(streams_of[3], (PREFIX // PAGE, KVH, OUT), 0, HD), jax.random.fold_in(streams_of[3], 1), 0, HD - 1).astype(jnp.int32)
    outlier_val = scatter_about(streams_of[4], (PREFIX, KVH, OUT), 3.0, 12.0, ((0, 64), (1, 8)))
    value_codes = draw_value_codes(jax.random.fold_in(streams_of[12], 71), 0)
    value_scale = jnp.clip(jnp.exp(math.log(0.03) - 1.7917595 * jax.random.uniform(streams_of[6], (PREFIX // PAGE, KVH, HD), jnp.float32) ** steps_of(streams_of[6], (PREFIX // PAGE, KVH, HD), ((0, 64), (1, 8)), -0.2, 0.2)), 0.005, 0.03)
    suffix_keys = scatter_about(streams_of[7], (POOLS, SPAGE, KVH, HD), 2.0, 10.0, ((0, 64), (2, 8)))
    suffix_values = scatter_about(streams_of[8], (POOLS, SPAGE, KVH, HD), 1.0, 6.0, ((0, 64), (2, 8)))
    page_table = draw_page_table(jax.random.fold_in(streams_of[12], 71), 0)
    suffix_len = draw_suffix_len(jax.random.fold_in(streams_of[12], 71), 0)
    out_weight = scatter_about(streams_of[11], (QH * HD, D), HD ** -0.5, 0.5, ((0, 8), (1, 64)))
    return {"queries": queries, "key_codes": key_codes, "key_scale": key_scale, "outlier_chan": outlier_chan, "outlier_val": outlier_val, "value_codes": value_codes, "value_scale": value_scale, "suffix_keys": suffix_keys, "suffix_values": suffix_values, "page_table": page_table, "suffix_len": suffix_len, "out_weight": out_weight}


def dequantize(code_block, scale_block, channels, corrections):
    page_count = scale_block.shape[0]
    page_rows = code_block.shape[0] // page_count
    groups = code_block.shape[1]
    head_size = code_block.shape[2]
    slots = channels.shape[2]
    onehot = (channels[..., None] == jnp.arange(head_size, dtype=jnp.int32)).astype(jnp.float32)
    correction = jnp.einsum('ptgo,pgoc->ptgc', corrections.reshape(page_count, page_rows, groups, slots).astype(jnp.float32), onehot)
    base = code_block.reshape(page_count, page_rows, groups, head_size).astype(jnp.float32) * scale_block[:, None]
    return (base + correction).reshape(code_block.shape).astype(jnp.bfloat16)

def dequantize_plain(code_block, scale_block):
    page_count = scale_block.shape[0]
    page_rows = code_block.shape[0] // page_count
    base = code_block.reshape(page_count, page_rows, code_block.shape[1], code_block.shape[2]).astype(jnp.float32) * scale_block[:, None]
    return base.reshape(code_block.shape).astype(jnp.bfloat16)

def reference(queries, key_codes, key_scale, outlier_chan, outlier_val, value_codes, value_scale, suffix_keys, suffix_values, page_table, suffix_len, out_weight):
    score_scale = 1.0 / math.sqrt(HD)
    query_groups = queries.astype(jnp.float32).reshape(B, KVH, QPK, HD)
    block_rows = math.gcd(PREFIX, 2048)
    block_pages = block_rows // PAGE
    block_count = PREFIX // block_rows

    def key_block_at(block_index):
        first_key = (block_index * block_rows).astype(jnp.int32)
        first_page = (block_index * block_pages).astype(jnp.int32)
        return dequantize(lax.dynamic_slice_in_dim(key_codes, first_key, block_rows, 0), lax.dynamic_slice_in_dim(key_scale, first_page, block_pages, 0), lax.dynamic_slice_in_dim(outlier_chan, first_page, block_pages, 0), lax.dynamic_slice_in_dim(outlier_val, first_key, block_rows, 0))

    def value_block_at(block_index):
        first_key = (block_index * block_rows).astype(jnp.int32)
        first_page = (block_index * block_pages).astype(jnp.int32)
        return dequantize_plain(lax.dynamic_slice_in_dim(value_codes, first_key, block_rows, 0), lax.dynamic_slice_in_dim(value_scale, first_page, block_pages, 0))

    def peak_pass(running, block_index):
        key_block = key_block_at(block_index)
        scores = jnp.einsum('bgqc,tgc->bgqt', query_groups, key_block.astype(jnp.float32)) * score_scale
        return (jnp.maximum(running, lax.optimization_barrier(jnp.max(scores, axis=-1))), None)
    indices = jnp.arange(block_count, dtype=jnp.int32)
    start_peak = jnp.full((B, KVH, QPK), -1e+30, dtype=jnp.float32)
    prefix_peak, ignored = lax.scan(peak_pass, start_peak, indices)
    pool_index = (jnp.arange(B, dtype=jnp.int32) // B_DEV)[:, None] * POOL + page_table
    sample_keys = suffix_keys[pool_index].reshape(B, S_MAX, KVH, HD)
    sample_values = suffix_values[pool_index].reshape(B, S_MAX, KVH, HD)
    live = jnp.arange(S_MAX, dtype=jnp.int32)[None, :] < suffix_len[:, None]
    suffix_scores = jnp.einsum('bgqc,bsgc->bgqs', query_groups, sample_keys.astype(jnp.float32)) * score_scale
    suffix_scores = jnp.where(live[:, None, None, :], suffix_scores, -1e+30)
    best = jnp.maximum(prefix_peak, lax.optimization_barrier(jnp.max(suffix_scores, axis=-1)))

    def value_pass(running, block_index):
        weight_sum, weighted = running
        key_block = key_block_at(block_index)
        value_block = value_block_at(block_index)
        scores = jnp.einsum('bgqc,tgc->bgqt', query_groups, key_block.astype(jnp.float32)) * score_scale
        weights = jnp.exp(scores - best[..., None])
        rounded = lax.optimization_barrier(weights.astype(jnp.bfloat16)).astype(jnp.float32)
        weight_sum = weight_sum + lax.optimization_barrier(jnp.sum(weights, axis=-1))
        weighted = weighted + jnp.einsum('bgqt,tgc->bgqc', rounded, value_block.astype(jnp.float32))
        return ((weight_sum, weighted), None)
    start_state = (jnp.zeros((B, KVH, QPK), jnp.float32), jnp.zeros((B, KVH, QPK, HD), jnp.float32))
    (weight_sum, weighted), ignored = lax.scan(value_pass, start_state, indices)
    suffix_weights = jnp.exp(suffix_scores - best[..., None])
    suffix_rounded = lax.optimization_barrier(suffix_weights.astype(jnp.bfloat16)).astype(jnp.float32)
    weight_sum = weight_sum + lax.optimization_barrier(jnp.sum(suffix_weights, axis=-1))
    weighted = weighted + jnp.einsum('bgqs,bsgc->bgqc', suffix_rounded, sample_values.astype(jnp.float32))
    attention = (weighted / weight_sum[..., None]).astype(jnp.bfloat16).reshape(B, QH * HD)
    return jnp.dot(attention, out_weight, preferred_element_type=jnp.float32).astype(jnp.bfloat16)
```

```python
import functools
import math

import jax
import jax.numpy as jnp
from jax import lax
from jax.experimental import pallas as pl
from jax.experimental.pallas import tpu as pltpu
from jax.sharding import Mesh, PartitionSpec as P

F32 = jnp.float32
BF16 = jnp.bfloat16
LANES = 128
HEADS = 8
PAGE = 128
TILE = 256
BLOCK = 1024
SPLIT = 32
STATS = 16
LOW = -1e30
VMEM = pl.BlockSpec(memory_space=pltpu.VMEM)
SMEM = pl.BlockSpec(memory_space=pltpu.SMEM)
ANY = pl.BlockSpec(memory_space=pl.ANY)
LIMIT = 48 * 1024 * 1024


def nt(a, b):
    return lax.dot_general(a, b, (((1,), (1,)), ((), ())), preferred_element_type=F32)


def split_rows(row):
    high = row.astype(BF16).astype(F32)
    rest = row - high
    middle = rest.astype(BF16).astype(F32)
    low = rest - middle
    part = lax.broadcasted_iota(jnp.int32, row.shape, row.ndim - 1) // SPLIT
    kept = jnp.where(part == 0, high, jnp.where(part == 1, middle, low))
    return jnp.where(part < 3, kept, 0.0).astype(BF16)


def to_lanes(columns):
    row = lax.broadcasted_iota(jnp.int32, columns.shape, 0)
    lane = lax.broadcasted_iota(jnp.int32, columns.shape, 1)
    return jnp.sum(jnp.where(lane % SPLIT == row, columns, 0.0), axis=0, keepdims=True)


def to_rows(stat):
    wide = jnp.broadcast_to(stat, (SPLIT, LANES))
    row = lax.broadcasted_iota(jnp.int32, wide.shape, 0)
    lane = lax.broadcasted_iota(jnp.int32, wide.shape, 1)
    return jnp.sum(jnp.where(lane % SPLIT == row, wide, 0.0), axis=1, keepdims=True)


def attend_kernel(
    own_ref,
    len_ref,
    table_ref,
    q_ref,
    own_q_ref,
    kscale_ref,
    chan_ref,
    outlier_ref,
    vscale_ref,
    kcodes_hbm,
    vcodes_hbm,
    skeys_hbm,
    svalues_hbm,
    out_ref,
    kbuf,
    vbuf,
    skbuf,
    svbuf,
    scores,
    peak,
    total,
    acc,
    ksem,
    vsem,
    ssem,
):
    keys = kbuf.shape[0]
    blocks = keys // BLOCK
    queries = q_ref.shape[0]
    score_scale = math.log2(math.e) / math.sqrt(LANES)

    def chunk(hbm, buf, sem, i):
        rows = pl.ds(pl.multiple_of(i * BLOCK, BLOCK), BLOCK)
        return pltpu.make_async_copy(hbm.at[rows, :], buf.at[rows, :], sem.at[i])

    for i in range(blocks):
        chunk(kcodes_hbm, kbuf, ksem, i).start()
    skeys = pltpu.make_async_copy(skeys_hbm, skbuf, ssem.at[0])
    svalues = pltpu.make_async_copy(svalues_hbm, svbuf, ssem.at[1])
    skeys.start()
    svalues.start()
    for i in range(blocks):
        chunk(vcodes_hbm, vbuf, vsem, i).start()

    peak[...] = jnp.full(peak.shape, LOW, F32)
    page_lane = lax.broadcasted_iota(jnp.int32, chan_ref.shape, 1)
    channel = lax.broadcasted_iota(jnp.int32, (HEADS, LANES), 1)

    @pl.loop(0, blocks)
    def score_block(i):
        chunk(kcodes_hbm, kbuf, ksem, i).wait()
        running = peak[...]
        for j in range(BLOCK // TILE):
            parts = []
            for p in range(TILE // PAGE):
                page = i * (BLOCK // PAGE) + j * (TILE // PAGE) + p
                rows = pl.ds(pl.multiple_of(page * PAGE, PAGE), PAGE)
                chosen = jnp.sum(
                    jnp.where(page_lane == page, chan_ref[...], 0), axis=1, keepdims=True
                )
                onehot = (channel == chosen).astype(BF16)
                correction = lax.dot_general(
                    outlier_ref[:, rows],
                    onehot,
                    (((0,), (0,)), ((), ())),
                    preferred_element_type=F32,
                )
                parts.append((kbuf[rows, :].astype(F32) * kscale_ref[page] + correction).astype(BF16))
            tile = nt(q_ref[...], jnp.concatenate(parts, axis=0))
            scores[i * (BLOCK // TILE) + j] = tile
            running = jnp.maximum(running, jnp.maximum(tile[:, :LANES], tile[:, LANES:]))
        peak[...] = running

    peak[...] = jnp.broadcast_to(
        jnp.max(peak[...], axis=1, keepdims=True) * score_scale, peak.shape
    )
    total[...] = jnp.zeros(total.shape, F32)
    acc[...] = jnp.zeros(acc.shape, F32)

    @pl.loop(0, blocks)
    def value_block(i):
        chunk(vcodes_hbm, vbuf, vsem, i).wait()
        running = total[...]
        top = peak[...]
        weights, values = [], []
        for j in range(BLOCK // TILE):
            for p in range(TILE // PAGE):
                page = i * (BLOCK // PAGE) + j * (TILE // PAGE) + p
                rows = pl.ds(pl.multiple_of(page * PAGE, PAGE), PAGE)
                values.append((vbuf[rows, :].astype(F32) * vscale_ref[page]).astype(BF16))
                part = scores[i * (BLOCK // TILE) + j, :, p * LANES : (p + 1) * LANES]
                weight = jnp.exp2(part * score_scale - top)
                running = running + weight
                weights.append(weight.astype(BF16))
        total[...] = running
        acc[...] += jnp.dot(
            jnp.concatenate(weights, axis=1),
            jnp.concatenate(values, axis=0),
            preferred_element_type=F32,
        )

    total[...] = jnp.broadcast_to(jnp.sum(total[...], axis=1, keepdims=True), total.shape)

    skeys.wait()
    svalues.wait()
    own = pl.ds(pl.multiple_of(own_ref[0] * HEADS, HEADS), HEADS)
    live = len_ref[0]
    place = lax.broadcasted_iota(jnp.int32, (HEADS, PAGE), 1)
    own_scores = [
        jnp.where(
            place + j * PAGE < live,
            nt(own_q_ref[...], skbuf[table_ref[0, j]]) * score_scale,
            LOW,
        )
        for j in range(skbuf.shape[0])
    ]
    top = peak[own, :]
    for part in own_scores:
        top = jnp.maximum(top, jnp.max(part, axis=1, keepdims=True))
    fade = jnp.exp2(peak[own, :] - top)
    sums = total[own, :] * fade
    weighted = acc[own, :] * fade
    for j, part in enumerate(own_scores):
        weight = jnp.where(place + j * PAGE < live, jnp.exp2(part - top), 0.0)
        sums = sums + jnp.sum(weight, axis=1, keepdims=True)
        weighted = weighted + jnp.dot(
            weight.astype(BF16), svbuf[table_ref[0, j]], preferred_element_type=F32
        )
    peak[own, :] = top
    total[own, :] = sums
    acc[own, :] = weighted

    for z in range(queries // SPLIT):
        rows = slice(z * SPLIT, (z + 1) * SPLIT)
        out_ref[z, :SPLIT, :] = (acc[rows, :] / total[rows, :]).astype(BF16)
        stat = split_rows(to_lanes(peak[rows, :] + jnp.log2(total[rows, :])))
        out_ref[z, SPLIT:, :] = jnp.broadcast_to(stat, (STATS, LANES))


def merge_kernel(in_ref, out_ref):
    sources = in_ref.shape[0]
    logs = [to_rows(in_ref[s, SPLIT:, :].astype(F32)[:1]) for s in range(sources)]
    top = functools.reduce(jnp.maximum, logs)
    sums = jnp.zeros(top.shape, F32)
    weighted = jnp.zeros((SPLIT, LANES), F32)
    for s in range(sources):
        weight = jnp.exp2(logs[s] - top)
        sums = sums + weight
        weighted = weighted + in_ref[s, :SPLIT, :].astype(F32) * weight
    merged = (weighted / sums).astype(BF16)
    copies, rows, lanes = out_ref.shape
    if rows > SPLIT:
        wide = jnp.broadcast_to(top + jnp.log2(sums), (SPLIT, LANES))
        stat = jnp.broadcast_to(split_rows(to_lanes(wide)), (STATS, LANES))
    for c in range(copies):
        out_ref[c, :SPLIT, :] = merged
        if rows > SPLIT:
            out_ref[c, SPLIT:, :] = stat


def project_kernel(in_ref, weight_ref, out_ref, wide):
    blocks = in_ref.shape[0]
    for z in range(blocks):
        wide[z * SPLIT : (z + 1) * SPLIT, :] = in_ref[z].astype(F32)
    samples = blocks * SPLIT // HEADS
    result = jnp.zeros((samples, LANES), F32)
    for h in range(HEADS):
        part = wide[pl.ds(h, samples, stride=HEADS), :].astype(BF16)
        result = result + jnp.dot(
            part, weight_ref[h * LANES : (h + 1) * LANES, :], preferred_element_type=F32
        )
    out_ref[...] = result.astype(BF16)


def sum_kernel(in_ref, out_ref):
    result = in_ref[0].astype(F32)
    for c in range(1, in_ref.shape[0]):
        result = result + in_ref[c].astype(F32)
    out_ref[...] = result.astype(BF16)


def spread(block, axis):
    copies = jnp.broadcast_to(block[None], (lax.axis_size(axis),) + block.shape)
    return lax.all_to_all(copies, axis, 0, 0)


def attend(
    own,
    all_queries,
    queries,
    key_codes,
    key_scale,
    outlier_chan,
    outlier_val,
    value_codes,
    value_scale,
    suffix_keys,
    suffix_values,
    page_table,
    suffix_len,
    depth,
):
    rows = all_queries.shape[0]
    keys = key_codes.shape[0]
    pools = suffix_keys.shape[0]
    params = pltpu.CompilerParams(vmem_limit_bytes=LIMIT)
    return pl.pallas_call(
        attend_kernel,
        out_shape=jax.ShapeDtypeStruct((depth, SPLIT + STATS, LANES), BF16),
        in_specs=[SMEM] * 3 + [VMEM] * 6 + [ANY] * 4,
        out_specs=VMEM,
        scratch_shapes=[
            pltpu.VMEM((keys, LANES), BF16),
            pltpu.VMEM((keys, LANES), BF16),
            pltpu.VMEM((pools, PAGE, LANES), BF16),
            pltpu.VMEM((pools, PAGE, LANES), BF16),
            pltpu.VMEM((keys // TILE, rows, TILE), F32),
            pltpu.VMEM((rows, LANES), F32),
            pltpu.VMEM((rows, LANES), F32),
            pltpu.VMEM((rows, LANES), F32),
            pltpu.SemaphoreType.DMA((keys // BLOCK,)),
            pltpu.SemaphoreType.DMA((keys // BLOCK,)),
            pltpu.SemaphoreType.DMA((2,)),
        ],
        compiler_params=params,
        name="attend",
    )(
        own,
        suffix_len,
        page_table,
        all_queries,
        queries,
        key_scale,
        outlier_chan.reshape(-1, HEADS).T,
        outlier_val.reshape(-1, HEADS).T,
        value_scale,
        key_codes.reshape(keys, LANES),
        value_codes.reshape(keys, LANES),
        suffix_keys.reshape(pools, PAGE, LANES),
        suffix_values.reshape(pools, PAGE, LANES),
    )


def shards(
    queries,
    key_codes,
    key_scale,
    outlier_chan,
    outlier_val,
    value_codes,
    value_scale,
    suffix_keys,
    suffix_values,
    page_table,
    suffix_len,
    out_weight,
):
    depth, width = lax.axis_size("z"), lax.axis_size("y")
    samples = depth * width
    queries = queries.reshape(HEADS, LANES)
    all_queries = spread(spread(queries, "y"), "z").reshape(samples * HEADS, LANES)
    own = (lax.axis_index("z") * width + lax.axis_index("y")).astype(jnp.int32).reshape(1)
    params = pltpu.CompilerParams(vmem_limit_bytes=LIMIT)
    partial = attend(
        own,
        all_queries,
        queries,
        key_codes,
        key_scale,
        outlier_chan,
        outlier_val,
        value_codes,
        value_scale,
        suffix_keys,
        suffix_values,
        page_table,
        suffix_len,
        depth,
    )
    partial = lax.all_to_all(partial, "z", 0, 0)
    partial = pl.pallas_call(
        merge_kernel,
        out_shape=jax.ShapeDtypeStruct((width, SPLIT + STATS, LANES), BF16),
        in_specs=[VMEM],
        out_specs=VMEM,
        compiler_params=params,
        name="merge_z",
    )(partial)
    partial = lax.all_to_all(partial, "y", 0, 0)
    attention = pl.pallas_call(
        merge_kernel,
        out_shape=jax.ShapeDtypeStruct((depth, SPLIT, LANES), BF16),
        in_specs=[VMEM],
        out_specs=VMEM,
        compiler_params=params,
        name="merge_y",
    )(partial)
    attention = lax.all_to_all(attention, "z", 0, 0)
    product = pl.pallas_call(
        project_kernel,
        out_shape=jax.ShapeDtypeStruct((samples, LANES), BF16),
        in_specs=[VMEM, VMEM],
        out_specs=VMEM,
        scratch_shapes=[pltpu.VMEM((samples * HEADS, LANES), F32)],
        compiler_params=params,
        name="project",
    )(attention, out_weight)
    tp = lax.axis_size("x") * lax.axis_size("core")
    product = lax.all_to_all(product.reshape(tp, samples // tp, LANES), ("x", "core"), 0, 0)
    return pl.pallas_call(
        sum_kernel,
        out_shape=jax.ShapeDtypeStruct((samples // tp, LANES), BF16),
        in_specs=[VMEM],
        out_specs=VMEM,
        compiler_params=params,
        name="sum_tp",
    )(product)


def solution(mesh):
    grid = Mesh(mesh.devices.reshape(16, 4, 4, 2), ("z", "y", "x", "core"))
    seq, tp = ("z", "y"), ("x", "core")
    return jax.shard_map(
        shards,
        mesh=grid,
        in_specs=(
            P(seq, tp, None),
            P(seq, tp, None),
            P(seq, tp, None),
            P(seq, tp, None),
            P(seq, tp, None),
            P(seq, tp, None),
            P(seq, tp, None),
            P(seq, None, tp, None),
            P(seq, None, tp, None),
            P(seq, None),
            P(seq),
            P(tp, seq),
        ),
        out_specs=P(tp, seq),
        check_vma=False,
    )
```

```python
import functools
import math

import jax
import jax.numpy as jnp
from jax import lax
from jax.experimental import pallas as pl
from jax.experimental.pallas import tpu as pltpu
from jax.sharding import Mesh, PartitionSpec as P

F32 = jnp.float32
BF16 = jnp.bfloat16
LANES = 128
HEADS = 8
PAGE = 128
TILE = 256
BLOCK = 1024
SPLIT = 32
STATS = 16
LOW = -1e30
VMEM = pl.BlockSpec(memory_space=pltpu.VMEM)
SMEM = pl.BlockSpec(memory_space=pltpu.SMEM)
HBM = pl.BlockSpec(memory_space=pltpu.HBM)
LIMIT = 60 * 1024 * 1024
SMALL = 4 * 1024 * 1024


def nt(a, b):
    return lax.dot_general(a, b, (((1,), (1,)), ((), ())), preferred_element_type=F32)


def split_rows(row):
    high = row.astype(BF16).astype(F32)
    rest = row - high
    middle = rest.astype(BF16).astype(F32)
    low = rest - middle
    part = lax.broadcasted_iota(jnp.int32, row.shape, row.ndim - 1) // SPLIT
    kept = jnp.where(part == 0, high, jnp.where(part == 1, middle, low))
    return jnp.where(part < 3, kept, 0.0).astype(BF16)


def to_lanes(columns):
    row = lax.broadcasted_iota(jnp.int32, columns.shape, 0)
    lane = lax.broadcasted_iota(jnp.int32, columns.shape, 1)
    return jnp.sum(jnp.where(lane % SPLIT == row, columns, 0.0), axis=0, keepdims=True)


def to_rows(stat):
    wide = jnp.broadcast_to(stat, (SPLIT, LANES))
    row = lax.broadcasted_iota(jnp.int32, wide.shape, 0)
    lane = lax.broadcasted_iota(jnp.int32, wide.shape, 1)
    return jnp.sum(jnp.where(lane % SPLIT == row, wide, 0.0), axis=1, keepdims=True)


def attend_kernel(
    own_ref,
    q_ref,
    len_hbm,
    table_hbm,
    own_q_hbm,
    kscale_hbm,
    chan_hbm,
    outlier_hbm,
    vscale_hbm,
    kcodes_hbm,
    vcodes_hbm,
    skeys_hbm,
    svalues_hbm,
    out_ref,
    len_ref,
    table_ref,
    own_q_ref,
    kscale_ref,
    chan_ref,
    outlier_ref,
    vscale_ref,
    kbuf,
    vbuf,
    skbuf,
    svbuf,
    scores,
    peak,
    total,
    acc,
    ksem,
    vsem,
    sem,
):
    keys = kbuf.shape[0]
    blocks = keys // BLOCK
    queries = q_ref.shape[0]
    score_scale = math.log2(math.e) / math.sqrt(LANES)

    def chunk(hbm, buf, sem, i):
        rows = pl.ds(pl.multiple_of(i * BLOCK, BLOCK), BLOCK)
        return pltpu.make_async_copy(hbm.at[rows, :], buf.at[rows, :], sem.at[i])

    first = [
        pltpu.make_async_copy(source, target, sem.at[n])
        for n, (source, target) in enumerate(
            ((kscale_hbm, kscale_ref), (chan_hbm, chan_ref), (outlier_hbm, outlier_ref))
        )
    ]
    second = [
        pltpu.make_async_copy(source, target, sem.at[3 + n])
        for n, (source, target) in enumerate(
            (
                (vscale_hbm, vscale_ref),
                (own_q_hbm, own_q_ref),
                (skeys_hbm, skbuf),
                (svalues_hbm, svbuf),
                (len_hbm, len_ref),
                (table_hbm, table_ref),
            )
        )
    ]
    for copy in first:
        copy.start()
    for i in range(blocks):
        chunk(kcodes_hbm, kbuf, ksem, i).start()
    for copy in second:
        copy.start()
    for i in range(blocks):
        chunk(vcodes_hbm, vbuf, vsem, i).start()

    peak[...] = jnp.full(peak.shape, LOW, F32)
    page_lane = lax.broadcasted_iota(jnp.int32, chan_ref.shape, 1)
    channel = lax.broadcasted_iota(jnp.int32, (HEADS, LANES), 1)

    for copy in first:
        copy.wait()

    @pl.loop(0, blocks)
    def score_block(i):
        chunk(kcodes_hbm, kbuf, ksem, i).wait()
        running = peak[...]
        for j in range(BLOCK // TILE):
            parts = []
            for p in range(TILE // PAGE):
                page = i * (BLOCK // PAGE) + j * (TILE // PAGE) + p
                rows = pl.ds(pl.multiple_of(page * PAGE, PAGE), PAGE)
                chosen = jnp.sum(
                    jnp.where(page_lane == page, chan_ref[...], 0), axis=1, keepdims=True
                )
                onehot = (channel == chosen).astype(BF16)
                correction = lax.dot_general(
                    outlier_ref[:, rows],
                    onehot,
                    (((0,), (0,)), ((), ())),
                    preferred_element_type=F32,
                )
                parts.append((kbuf[rows, :].astype(F32) * kscale_ref[page] + correction).astype(BF16))
            tile = nt(q_ref[...], jnp.concatenate(parts, axis=0))
            scores[i * (BLOCK // TILE) + j] = tile
            running = jnp.maximum(running, jnp.maximum(tile[:, :LANES], tile[:, LANES:]))
        peak[...] = running

    peak[...] = jnp.broadcast_to(
        jnp.max(peak[...], axis=1, keepdims=True) * score_scale, peak.shape
    )
    total[...] = jnp.zeros(total.shape, F32)
    acc[...] = jnp.zeros(acc.shape, F32)
    for copy in second:
        copy.wait()

    @pl.loop(0, blocks)
    def value_block(i):
        chunk(vcodes_hbm, vbuf, vsem, i).wait()
        running = total[...]
        top = peak[...]
        weights, values = [], []
        for j in range(BLOCK // TILE):
            for p in range(TILE // PAGE):
                page = i * (BLOCK // PAGE) + j * (TILE // PAGE) + p
                rows = pl.ds(pl.multiple_of(page * PAGE, PAGE), PAGE)
                values.append((vbuf[rows, :].astype(F32) * vscale_ref[page]).astype(BF16))
                part = scores[i * (BLOCK // TILE) + j, :, p * LANES : (p + 1) * LANES]
                weight = jnp.exp2(part * score_scale - top)
                running = running + weight
                weights.append(weight.astype(BF16))
        total[...] = running
        acc[...] += jnp.dot(
            jnp.concatenate(weights, axis=1),
            jnp.concatenate(values, axis=0),
            preferred_element_type=F32,
        )

    total[...] = jnp.broadcast_to(jnp.sum(total[...], axis=1, keepdims=True), total.shape)

    own = pl.ds(pl.multiple_of(own_ref[0] * HEADS, HEADS), HEADS)
    live = len_ref[0]
    place = lax.broadcasted_iota(jnp.int32, (HEADS, PAGE), 1)
    own_scores = [
        jnp.where(
            place + j * PAGE < live,
            nt(own_q_ref[...], skbuf[table_ref[0, j]]) * score_scale,
            LOW,
        )
        for j in range(skbuf.shape[0])
    ]
    top = peak[own, :]
    for part in own_scores:
        top = jnp.maximum(top, jnp.max(part, axis=1, keepdims=True))
    fade = jnp.exp2(peak[own, :] - top)
    sums = total[own, :] * fade
    weighted = acc[own, :] * fade
    for j, part in enumerate(own_scores):
        weight = jnp.where(place + j * PAGE < live, jnp.exp2(part - top), 0.0)
        sums = sums + jnp.sum(weight, axis=1, keepdims=True)
        weighted = weighted + jnp.dot(
            weight.astype(BF16), svbuf[table_ref[0, j]], preferred_element_type=F32
        )
    peak[own, :] = top
    total[own, :] = sums
    acc[own, :] = weighted

    pieces = out_ref.shape[0]
    stride = queries // SPLIT * HEADS
    for c in range(pieces):
        rows = [
            slice(u * stride + c * HEADS, u * stride + (c + 1) * HEADS)
            for u in range(SPLIT // HEADS)
        ]
        part = [acc[r, :] / total[r, :] for r in rows]
        logs = [peak[r, :] + jnp.log2(total[r, :]) for r in rows]
        out_ref[c, :SPLIT, :] = jnp.concatenate(part, axis=0).astype(BF16)
        stat = split_rows(to_lanes(jnp.concatenate(logs, axis=0)))
        out_ref[c, SPLIT:, :] = jnp.broadcast_to(stat, (STATS, LANES))


def merge_kernel(in_ref, out_ref):
    sources = in_ref.shape[0]
    logs = [to_rows(in_ref[s, SPLIT:, :].astype(F32)[:1]) for s in range(sources)]
    top = functools.reduce(jnp.maximum, logs)
    sums = jnp.zeros(top.shape, F32)
    weighted = jnp.zeros((SPLIT, LANES), F32)
    for s in range(sources):
        weight = jnp.exp2(logs[s] - top)
        sums = sums + weight
        weighted = weighted + in_ref[s, :SPLIT, :].astype(F32) * weight
    merged = (weighted / sums).astype(BF16)
    copies, rows, lanes = out_ref.shape
    if rows > SPLIT:
        wide = jnp.broadcast_to(top + jnp.log2(sums), (SPLIT, LANES))
        stat = jnp.broadcast_to(split_rows(to_lanes(wide)), (STATS, LANES))
    for c in range(copies):
        out_ref[c, :SPLIT, :] = merged
        if rows > SPLIT:
            out_ref[c, SPLIT:, :] = stat


def project_kernel(in_ref, weight_ref, out_ref, wide):
    blocks = in_ref.shape[0]
    for c in range(blocks):
        block = in_ref[c].astype(F32)
        for u in range(SPLIT // HEADS):
            first = (u * blocks + c) * HEADS
            wide[first : first + HEADS, :] = block[u * HEADS : (u + 1) * HEADS]
    samples = blocks * SPLIT // HEADS
    result = jnp.zeros((samples, LANES), F32)
    for h in range(HEADS):
        part = wide[pl.ds(h, samples, stride=HEADS), :].astype(BF16)
        result = result + jnp.dot(
            part, weight_ref[h * LANES : (h + 1) * LANES, :], preferred_element_type=F32
        )
    out_ref[...] = result.astype(BF16)


def sum_kernel(in_ref, out_ref):
    result = in_ref[0].astype(F32)
    for c in range(1, in_ref.shape[0]):
        result = result + in_ref[c].astype(F32)
    out_ref[...] = result.astype(BF16)


def spread(block, axis):
    copies = jnp.broadcast_to(block[None], (lax.axis_size(axis),) + block.shape)
    return lax.all_to_all(copies, axis, 0, 0)


def attend(
    own,
    all_queries,
    queries,
    key_codes,
    key_scale,
    outlier_chan,
    outlier_val,
    value_codes,
    value_scale,
    suffix_keys,
    suffix_values,
    page_table,
    suffix_len,
):
    rows = all_queries.shape[0]
    keys = key_codes.shape[0]
    pools = suffix_keys.shape[0]
    params = pltpu.CompilerParams(vmem_limit_bytes=LIMIT)
    return pl.pallas_call(
        attend_kernel,
        out_shape=jax.ShapeDtypeStruct((rows // SPLIT, SPLIT + STATS, LANES), BF16),
        in_specs=[SMEM, VMEM] + [HBM] * 11,
        out_specs=VMEM,
        scratch_shapes=[
            pltpu.SMEM(suffix_len.shape, jnp.int32),
            pltpu.SMEM(page_table.shape, jnp.int32),
            pltpu.VMEM(queries.shape, BF16),
            pltpu.VMEM(key_scale.shape, F32),
            pltpu.VMEM((HEADS, keys // PAGE), jnp.int32),
            pltpu.VMEM((HEADS, keys), BF16),
            pltpu.VMEM(value_scale.shape, F32),
            pltpu.VMEM((keys, LANES), BF16),
            pltpu.VMEM((keys, LANES), BF16),
            pltpu.VMEM((pools, PAGE, LANES), BF16),
            pltpu.VMEM((pools, PAGE, LANES), BF16),
            pltpu.VMEM((keys // TILE, rows, TILE), F32),
            pltpu.VMEM((rows, LANES), F32),
            pltpu.VMEM((rows, LANES), F32),
            pltpu.VMEM((rows, LANES), F32),
            pltpu.SemaphoreType.DMA((keys // BLOCK,)),
            pltpu.SemaphoreType.DMA((keys // BLOCK,)),
            pltpu.SemaphoreType.DMA((9,)),
        ],
        compiler_params=params,
        name="attend",
    )(
        own,
        all_queries,
        suffix_len,
        page_table,
        queries,
        key_scale,
        outlier_chan.reshape(-1, HEADS).T,
        outlier_val.reshape(-1, HEADS).T,
        value_scale,
        key_codes.reshape(keys, LANES),
        value_codes.reshape(keys, LANES),
        suffix_keys.reshape(pools, PAGE, LANES),
        suffix_values.reshape(pools, PAGE, LANES),
    )


def shards(
    queries,
    key_codes,
    key_scale,
    outlier_chan,
    outlier_val,
    value_codes,
    value_scale,
    suffix_keys,
    suffix_values,
    page_table,
    suffix_len,
    out_weight,
):
    seq, near, far = ("zh", "zl", "y"), ("zl", "y"), "zh"
    samples = lax.axis_size(seq)
    queries = queries.reshape(HEADS, LANES)
    all_queries = spread(queries, seq).reshape(samples * HEADS, LANES)
    own = lax.axis_index(seq).astype(jnp.int32).reshape(1)
    params = pltpu.CompilerParams(vmem_limit_bytes=SMALL)
    partial = attend(
        own,
        all_queries,
        queries,
        key_codes,
        key_scale,
        outlier_chan,
        outlier_val,
        value_codes,
        value_scale,
        suffix_keys,
        suffix_values,
        page_table,
        suffix_len,
    )
    partial = lax.all_to_all(partial, near, 0, 0)
    partial = pl.pallas_call(
        merge_kernel,
        out_shape=jax.ShapeDtypeStruct((lax.axis_size(far), SPLIT + STATS, LANES), BF16),
        in_specs=[VMEM],
        out_specs=VMEM,
        compiler_params=params,
        name="merge_near",
    )(partial)
    partial = lax.all_to_all(partial, far, 0, 0)
    attention = pl.pallas_call(
        merge_kernel,
        out_shape=jax.ShapeDtypeStruct((lax.axis_size(near), SPLIT, LANES), BF16),
        in_specs=[VMEM],
        out_specs=VMEM,
        compiler_params=params,
        name="merge_far",
    )(partial)
    attention = lax.all_to_all(attention, near, 0, 0)
    product = pl.pallas_call(
        project_kernel,
        out_shape=jax.ShapeDtypeStruct((samples, LANES), BF16),
        in_specs=[VMEM, VMEM],
        out_specs=VMEM,
        scratch_shapes=[pltpu.VMEM((samples * HEADS, LANES), F32)],
        compiler_params=params,
        name="project",
    )(attention, out_weight)
    tp = lax.axis_size("x") * lax.axis_size("core")
    product = lax.all_to_all(product.reshape(tp, samples // tp, LANES), ("x", "core"), 0, 0)
    return pl.pallas_call(
        sum_kernel,
        out_shape=jax.ShapeDtypeStruct((samples // tp, LANES), BF16),
        in_specs=[VMEM],
        out_specs=VMEM,
        compiler_params=params,
        name="sum_tp",
    )(product)


def solution(mesh):
    grid = Mesh(mesh.devices.reshape(4, 4, 4, 4, 2), ("zh", "zl", "y", "x", "core"))
    seq, tp = ("zh", "zl", "y"), ("x", "core")
    return jax.shard_map(
        shards,
        mesh=grid,
        in_specs=(
            P(seq, tp, None),
            P(seq, tp, None),
            P(seq, tp, None),
            P(seq, tp, None),
            P(seq, tp, None),
            P(seq, tp, None),
            P(seq, tp, None),
            P(seq, None, tp, None),
            P(seq, None, tp, None),
            P(seq, None),
            P(seq),
            P(tp, seq),
        ),
        out_specs=P(tp, seq),
        check_vma=False,
    )
```

```python
import functools
import math

import jax
import jax.numpy as jnp
from jax import lax
from jax.experimental import pallas as pl
from jax.experimental.pallas import tpu as pltpu
from jax.sharding import Mesh, PartitionSpec as P

F32 = jnp.float32
BF16 = jnp.bfloat16
LANES = 128
HEADS = 8
PAGE = 128
TILE = 256
BLOCK = 1024
SPLIT = 32
STATS = 16
LOW = -1e30
VMEM = pl.BlockSpec(memory_space=pltpu.VMEM)
SMEM = pl.BlockSpec(memory_space=pltpu.SMEM)
HBM = pl.BlockSpec(memory_space=pltpu.HBM)
LIMIT = 60 * 1024 * 1024
SMALL = 4 * 1024 * 1024


def nt(a, b):
    return lax.dot_general(a, b, (((1,), (1,)), ((), ())), preferred_element_type=F32)


def split_rows(row):
    high = row.astype(BF16).astype(F32)
    rest = row - high
    middle = rest.astype(BF16).astype(F32)
    low = rest - middle
    part = lax.broadcasted_iota(jnp.int32, row.shape, row.ndim - 1) // SPLIT
    kept = jnp.where(part == 0, high, jnp.where(part == 1, middle, low))
    return jnp.where(part < 3, kept, 0.0).astype(BF16)


def to_lanes(columns):
    row = lax.broadcasted_iota(jnp.int32, columns.shape, 0)
    lane = lax.broadcasted_iota(jnp.int32, columns.shape, 1)
    return jnp.sum(jnp.where(lane % SPLIT == row, columns, 0.0), axis=0, keepdims=True)


def to_rows(stat):
    wide = jnp.broadcast_to(stat, (SPLIT, LANES))
    row = lax.broadcasted_iota(jnp.int32, wide.shape, 0)
    lane = lax.broadcasted_iota(jnp.int32, wide.shape, 1)
    return jnp.sum(jnp.where(lane % SPLIT == row, wide, 0.0), axis=1, keepdims=True)


def attend_kernel(
    own_ref,
    q_ref,
    len_hbm,
    table_hbm,
    own_q_hbm,
    kscale_hbm,
    chan_hbm,
    outlier_hbm,
    vscale_hbm,
    kcodes_hbm,
    vcodes_hbm,
    skeys_hbm,
    svalues_hbm,
    out_ref,
    len_ref,
    table_ref,
    own_q_ref,
    kscale_ref,
    chan_ref,
    outlier_ref,
    vscale_ref,
    kbuf,
    vbuf,
    skbuf,
    svbuf,
    scores,
    peak,
    total,
    acc,
    ksem,
    vsem,
    sem,
):
    keys = kbuf.shape[0]
    blocks = keys // BLOCK
    queries = q_ref.shape[0]
    score_scale = math.log2(math.e) / math.sqrt(LANES)

    def chunk(hbm, buf, sem, i):
        rows = pl.ds(pl.multiple_of(i * BLOCK, BLOCK), BLOCK)
        return pltpu.make_async_copy(hbm.at[rows, :], buf.at[rows, :], sem.at[i])

    first = [
        pltpu.make_async_copy(source, target, sem.at[n])
        for n, (source, target) in enumerate(
            ((kscale_hbm, kscale_ref), (chan_hbm, chan_ref), (outlier_hbm, outlier_ref))
        )
    ]
    second = [
        pltpu.make_async_copy(source, target, sem.at[3 + n])
        for n, (source, target) in enumerate(
            (
                (vscale_hbm, vscale_ref),
                (own_q_hbm, own_q_ref),
                (skeys_hbm, skbuf),
                (svalues_hbm, svbuf),
                (len_hbm, len_ref),
                (table_hbm, table_ref),
            )
        )
    ]
    for copy in first:
        copy.start()
    for i in range(blocks):
        chunk(kcodes_hbm, kbuf, ksem, i).start()
    for copy in second:
        copy.start()
    for i in range(blocks):
        chunk(vcodes_hbm, vbuf, vsem, i).start()

    peak[...] = jnp.full(peak.shape, LOW, F32)
    page_lane = lax.broadcasted_iota(jnp.int32, chan_ref.shape, 1)
    channel = lax.broadcasted_iota(jnp.int32, (HEADS, LANES), 1)

    for copy in first:
        copy.wait()

    @pl.loop(0, blocks)
    def score_block(i):
        chunk(kcodes_hbm, kbuf, ksem, i).wait()
        running = peak[...]
        for j in range(BLOCK // TILE):
            parts = []
            for p in range(TILE // PAGE):
                page = i * (BLOCK // PAGE) + j * (TILE // PAGE) + p
                rows = pl.ds(pl.multiple_of(page * PAGE, PAGE), PAGE)
                chosen = jnp.sum(
                    jnp.where(page_lane == page, chan_ref[...], 0), axis=1, keepdims=True
                )
                onehot = (channel == chosen).astype(BF16)
                correction = lax.dot_general(
                    outlier_ref[:, rows],
                    onehot,
                    (((0,), (0,)), ((), ())),
                    preferred_element_type=F32,
                )
                parts.append((kbuf[rows, :].astype(F32) * kscale_ref[page] + correction).astype(BF16))
            tile = nt(q_ref[...], jnp.concatenate(parts, axis=0))
            scores[i * (BLOCK // TILE) + j] = tile
            running = jnp.maximum(running, jnp.maximum(tile[:, :LANES], tile[:, LANES:]))
        peak[...] = running

    peak[...] = jnp.broadcast_to(
        jnp.max(peak[...], axis=1, keepdims=True) * score_scale, peak.shape
    )
    total[...] = jnp.zeros(total.shape, F32)
    acc[...] = jnp.zeros(acc.shape, F32)
    for copy in second:
        copy.wait()

    @pl.loop(0, blocks)
    def value_block(i):
        chunk(vcodes_hbm, vbuf, vsem, i).wait()
        running = total[...]
        top = peak[...]
        weights, values = [], []
        for j in range(BLOCK // TILE):
            for p in range(TILE // PAGE):
                page = i * (BLOCK // PAGE) + j * (TILE // PAGE) + p
                rows = pl.ds(pl.multiple_of(page * PAGE, PAGE), PAGE)
                values.append((vbuf[rows, :].astype(F32) * vscale_ref[page]).astype(BF16))
                part = scores[i * (BLOCK // TILE) + j, :, p * LANES : (p + 1) * LANES]
                weight = jnp.exp2(part * score_scale - top)
                running = running + weight
                weights.append(weight.astype(BF16))
        total[...] = running
        acc[...] += jnp.dot(
            jnp.concatenate(weights, axis=1),
            jnp.concatenate(values, axis=0),
            preferred_element_type=F32,
        )

    total[...] = jnp.broadcast_to(jnp.sum(total[...], axis=1, keepdims=True), total.shape)

    own = pl.ds(pl.multiple_of(own_ref[0] * HEADS, HEADS), HEADS)
    live = len_ref[0]
    place = lax.broadcasted_iota(jnp.int32, (HEADS, PAGE), 1)
    own_scores = [
        jnp.where(
            place + j * PAGE < live,
            nt(own_q_ref[...], skbuf[table_ref[0, j]]) * score_scale,
            LOW,
        )
        for j in range(skbuf.shape[0])
    ]
    top = peak[own, :]
    for part in own_scores:
        top = jnp.maximum(top, jnp.max(part, axis=1, keepdims=True))
    fade = jnp.exp2(peak[own, :] - top)
    sums = total[own, :] * fade
    weighted = acc[own, :] * fade
    for j, part in enumerate(own_scores):
        weight = jnp.where(place + j * PAGE < live, jnp.exp2(part - top), 0.0)
        sums = sums + jnp.sum(weight, axis=1, keepdims=True)
        weighted = weighted + jnp.dot(
            weight.astype(BF16), svbuf[table_ref[0, j]], preferred_element_type=F32
        )
    peak[own, :] = top
    total[own, :] = sums
    acc[own, :] = weighted

    pieces = out_ref.shape[0]
    stride = queries // SPLIT * HEADS
    for c in range(pieces):
        rows = [
            slice(u * stride + c * HEADS, u * stride + (c + 1) * HEADS)
            for u in range(SPLIT // HEADS)
        ]
        part = [acc[r, :] / total[r, :] for r in rows]
        logs = [peak[r, :] + jnp.log2(total[r, :]) for r in rows]
        out_ref[c, :SPLIT, :] = jnp.concatenate(part, axis=0).astype(BF16)
        stat = split_rows(to_lanes(jnp.concatenate(logs, axis=0)))
        out_ref[c, SPLIT:, :] = jnp.broadcast_to(stat, (STATS, LANES))


def merge_kernel(in_ref, out_ref):
    sources = in_ref.shape[0]
    logs = [to_rows(in_ref[s, SPLIT:, :].astype(F32)[:1]) for s in range(sources)]
    top = functools.reduce(jnp.maximum, logs)
    sums = jnp.zeros(top.shape, F32)
    weighted = jnp.zeros((SPLIT, LANES), F32)
    for s in range(sources):
        weight = jnp.exp2(logs[s] - top)
        sums = sums + weight
        weighted = weighted + in_ref[s, :SPLIT, :].astype(F32) * weight
    merged = (weighted / sums).astype(BF16)
    copies, rows, lanes = out_ref.shape
    if rows > SPLIT:
        wide = jnp.broadcast_to(top + jnp.log2(sums), (SPLIT, LANES))
        stat = jnp.broadcast_to(split_rows(to_lanes(wide)), (STATS, LANES))
    for c in range(copies):
        out_ref[c, :SPLIT, :] = merged
        if rows > SPLIT:
            out_ref[c, SPLIT:, :] = stat


def project_kernel(in_ref, weight_ref, out_ref, wide):
    blocks = in_ref.shape[0]
    for c in range(blocks):
        block = in_ref[c].astype(F32)
        for u in range(SPLIT // HEADS):
            first = (u * blocks + c) * HEADS
            wide[first : first + HEADS, :] = block[u * HEADS : (u + 1) * HEADS]
    samples = blocks * SPLIT // HEADS
    result = jnp.zeros((samples, LANES), F32)
    for h in range(HEADS):
        part = wide[pl.ds(h, samples, stride=HEADS), :].astype(BF16)
        result = result + jnp.dot(
            part, weight_ref[h * LANES : (h + 1) * LANES, :], preferred_element_type=F32
        )
    out_ref[...] = result.astype(BF16)


def sum_kernel(in_ref, out_ref):
    result = in_ref[0].astype(F32)
    for c in range(1, in_ref.shape[0]):
        result = result + in_ref[c].astype(F32)
    out_ref[...] = result.astype(BF16)


def spread(block, axis):
    copies = jnp.broadcast_to(block[None], (lax.axis_size(axis),) + block.shape)
    return lax.all_to_all(copies, axis, 0, 0)


def attend(
    own,
    all_queries,
    queries,
    key_codes,
    key_scale,
    outlier_chan,
    outlier_val,
    value_codes,
    value_scale,
    suffix_keys,
    suffix_values,
    page_table,
    suffix_len,
):
    rows = all_queries.shape[0]
    keys = key_codes.shape[0]
    pools = suffix_keys.shape[0]
    params = pltpu.CompilerParams(vmem_limit_bytes=LIMIT)
    return pl.pallas_call(
        attend_kernel,
        out_shape=jax.ShapeDtypeStruct((rows // SPLIT, SPLIT + STATS, LANES), BF16),
        in_specs=[SMEM, VMEM] + [HBM] * 11,
        out_specs=VMEM,
        scratch_shapes=[
            pltpu.SMEM(suffix_len.shape, jnp.int32),
            pltpu.SMEM(page_table.shape, jnp.int32),
            pltpu.VMEM(queries.shape, BF16),
            pltpu.VMEM(key_scale.shape, F32),
            pltpu.VMEM((HEADS, keys // PAGE), jnp.int32),
            pltpu.VMEM((HEADS, keys), BF16),
            pltpu.VMEM(value_scale.shape, F32),
            pltpu.VMEM((keys, LANES), BF16),
            pltpu.VMEM((keys, LANES), BF16),
            pltpu.VMEM((pools, PAGE, LANES), BF16),
            pltpu.VMEM((pools, PAGE, LANES), BF16),
            pltpu.VMEM((keys // TILE, rows, TILE), F32),
            pltpu.VMEM((rows, LANES), F32),
            pltpu.VMEM((rows, LANES), F32),
            pltpu.VMEM((rows, LANES), F32),
            pltpu.SemaphoreType.DMA((keys // BLOCK,)),
            pltpu.SemaphoreType.DMA((keys // BLOCK,)),
            pltpu.SemaphoreType.DMA((9,)),
        ],
        compiler_params=params,
        name="attend",
    )(
        own,
        all_queries,
        suffix_len,
        page_table,
        queries,
        key_scale,
        outlier_chan.reshape(-1, HEADS).T,
        outlier_val.reshape(-1, HEADS).T,
        value_scale,
        key_codes.reshape(keys, LANES),
        value_codes.reshape(keys, LANES),
        suffix_keys.reshape(pools, PAGE, LANES),
        suffix_values.reshape(pools, PAGE, LANES),
    )


def shards(
    queries,
    key_codes,
    key_scale,
    outlier_chan,
    outlier_val,
    value_codes,
    value_scale,
    suffix_keys,
    suffix_values,
    page_table,
    suffix_len,
    out_weight,
):
    seq, near, far = ("zh", "zl", "y"), ("zl", "y"), "zh"
    samples = lax.axis_size(seq)
    queries = queries.reshape(HEADS, LANES)
    own = lax.axis_index(seq).astype(jnp.int32).reshape(1)
    all_queries = spread(queries, seq).reshape(samples * HEADS, LANES)
    (
        own,
        queries,
        all_queries,
        key_codes,
        key_scale,
        outlier_chan,
        outlier_val,
        value_codes,
        value_scale,
        suffix_keys,
        suffix_values,
        page_table,
        suffix_len,
        out_weight,
    ) = lax.optimization_barrier(
        (
            own,
            queries,
            all_queries,
            key_codes,
            key_scale,
            outlier_chan,
            outlier_val,
            value_codes,
            value_scale,
            suffix_keys,
            suffix_values,
            page_table,
            suffix_len,
            out_weight,
        )
    )
    params = pltpu.CompilerParams(vmem_limit_bytes=SMALL)
    partial = attend(
        own,
        all_queries,
        queries,
        key_codes,
        key_scale,
        outlier_chan,
        outlier_val,
        value_codes,
        value_scale,
        suffix_keys,
        suffix_values,
        page_table,
        suffix_len,
    )
    partial = lax.all_to_all(partial, near, 0, 0)
    partial = pl.pallas_call(
        merge_kernel,
        out_shape=jax.ShapeDtypeStruct((lax.axis_size(far), SPLIT + STATS, LANES), BF16),
        in_specs=[VMEM],
        out_specs=VMEM,
        compiler_params=params,
        name="merge_near",
    )(partial)
    partial = lax.all_to_all(partial, far, 0, 0)
    attention = pl.pallas_call(
        merge_kernel,
        out_shape=jax.ShapeDtypeStruct((lax.axis_size(near), SPLIT, LANES), BF16),
        in_specs=[VMEM],
        out_specs=VMEM,
        compiler_params=params,
        name="merge_far",
    )(partial)
    attention = lax.all_to_all(attention, near, 0, 0)
    product = pl.pallas_call(
        project_kernel,
        out_shape=jax.ShapeDtypeStruct((samples, LANES), BF16),
        in_specs=[VMEM, VMEM],
        out_specs=VMEM,
        scratch_shapes=[pltpu.VMEM((samples * HEADS, LANES), F32)],
        compiler_params=params,
        name="project",
    )(attention, out_weight)
    tp = lax.axis_size("x") * lax.axis_size("core")
    product = lax.all_to_all(product.reshape(tp, samples // tp, LANES), ("x", "core"), 0, 0)
    return pl.pallas_call(
        sum_kernel,
        out_shape=jax.ShapeDtypeStruct((samples // tp, LANES), BF16),
        in_specs=[VMEM],
        out_specs=VMEM,
        compiler_params=params,
        name="sum_tp",
    )(product)


def solution(mesh):
    grid = Mesh(mesh.devices.reshape(4, 4, 4, 4, 2), ("zh", "zl", "y", "x", "core"))
    seq, tp = ("zh", "zl", "y"), ("x", "core")
    return jax.shard_map(
        shards,
        mesh=grid,
        in_specs=(
            P(seq, tp, None),
            P(seq, tp, None),
            P(seq, tp, None),
            P(seq, tp, None),
            P(seq, tp, None),
            P(seq, tp, None),
            P(seq, tp, None),
            P(seq, None, tp, None),
            P(seq, None, tp, None),
            P(seq, None),
            P(seq),
            P(tp, seq),
        ),
        out_specs=P(tp, seq),
        check_vma=False,
    )
```

```python
import functools
import math

import jax
import jax.numpy as jnp
from jax import lax
from jax.experimental import pallas as pl
from jax.experimental.pallas import tpu as pltpu
from jax.sharding import Mesh, PartitionSpec as P

F32 = jnp.float32
BF16 = jnp.bfloat16
LANES = 128
HEADS = 8
PAGE = 128
TILE = 256
BLOCK = 1024
PAGES = BLOCK // PAGE
SCORE_SCALE = math.log2(math.e) / math.sqrt(LANES)
SPLIT = 32
STATS = 16
LOW = -1e30
VMEM = pl.BlockSpec(memory_space=pltpu.VMEM)
SMEM = pl.BlockSpec(memory_space=pltpu.SMEM)
HBM = pl.BlockSpec(memory_space=pltpu.HBM)
PREPARE_LIMIT = 57 * 1024 * 1024
ATTEND_LIMIT = 57 * 1024 * 1024
SMALL = 4 * 1024 * 1024


def nt(a, b):
    return lax.dot_general(a, b, (((1,), (1,)), ((), ())), preferred_element_type=F32)


def split_rows(row):
    high = row.astype(BF16).astype(F32)
    rest = row - high
    middle = rest.astype(BF16).astype(F32)
    low = rest - middle
    part = lax.broadcasted_iota(jnp.int32, row.shape, row.ndim - 1) // SPLIT
    kept = jnp.where(part == 0, high, jnp.where(part == 1, middle, low))
    return jnp.where(part < 3, kept, 0.0).astype(BF16)


def to_lanes(columns):
    row = lax.broadcasted_iota(jnp.int32, columns.shape, 0)
    lane = lax.broadcasted_iota(jnp.int32, columns.shape, 1)
    return jnp.sum(jnp.where(lane % SPLIT == row, columns, 0.0), axis=0, keepdims=True)


def to_rows(stat):
    wide = jnp.broadcast_to(stat, (SPLIT, LANES))
    row = lax.broadcasted_iota(jnp.int32, wide.shape, 0)
    lane = lax.broadcasted_iota(jnp.int32, wide.shape, 1)
    return jnp.sum(jnp.where(lane % SPLIT == row, wide, 0.0), axis=1, keepdims=True)


def prepare_kernel(
    len_hbm,
    table_hbm,
    own_q_hbm,
    kscale_hbm,
    chan_hbm,
    outlier_hbm,
    vscale_hbm,
    kcodes_hbm,
    vcodes_hbm,
    skeys_hbm,
    svalues_hbm,
    keys_ref,
    values_ref,
    own_ref,
    len_ref,
    table_ref,
    own_q_ref,
    kscale_ref,
    chan_ref,
    outlier_ref,
    vscale_ref,
    skbuf,
    svbuf,
    onehot,
    ksem,
    vsem,
    sem,
):
    blocks = keys_ref.shape[0] // BLOCK

    def chunk(hbm, buf, sems, i):
        rows = pl.ds(pl.multiple_of(i * BLOCK, BLOCK), BLOCK)
        return pltpu.make_async_copy(hbm.at[rows, :], buf.at[rows, :], sems.at[i])

    small = [
        pltpu.make_async_copy(source, target, sem.at[n])
        for n, (source, target) in enumerate(
            (
                (chan_hbm, chan_ref),
                (outlier_hbm, outlier_ref),
                (kscale_hbm, kscale_ref),
                (vscale_hbm, vscale_ref),
                (own_q_hbm, own_q_ref),
                (skeys_hbm, skbuf),
                (svalues_hbm, svbuf),
                (len_hbm, len_ref),
                (table_hbm, table_ref),
            )
        )
    ]
    for copy in small:
        copy.start()
    for i in range(blocks):
        chunk(kcodes_hbm, keys_ref, ksem, i).start()
    for i in range(blocks):
        chunk(vcodes_hbm, values_ref, vsem, i).start()
    for copy in small:
        copy.wait()

    lane = lax.broadcasted_iota(jnp.int32, (HEADS, LANES), 1)
    channels = chan_ref[...]
    for page in range(onehot.shape[0]):
        onehot[page] = (lane == channels[:, page : page + 1]).astype(F32)

    live = len_ref[0]
    own_scores = [
        jnp.where(
            lane + j * PAGE < live,
            nt(own_q_ref[...], skbuf[table_ref[0, j]]) * SCORE_SCALE,
            LOW,
        )
        for j in range(skbuf.shape[0])
    ]
    top = functools.reduce(jnp.maximum, own_scores)
    top = jnp.max(top, axis=1, keepdims=True)
    sums = jnp.zeros((HEADS, LANES), F32)
    weighted = jnp.zeros((HEADS, LANES), F32)
    for j, part in enumerate(own_scores):
        weight = jnp.where(lane + j * PAGE < live, jnp.exp2(part - top), 0.0)
        sums = sums + weight
        weighted = weighted + jnp.dot(
            weight.astype(BF16), svbuf[table_ref[0, j]], preferred_element_type=F32
        )
    own_ref[0] = jnp.broadcast_to(top, (HEADS, LANES))
    own_ref[1] = jnp.broadcast_to(jnp.sum(sums, axis=1, keepdims=True), (HEADS, LANES))
    own_ref[2] = weighted
    none = jnp.zeros((HEADS, LANES), F32)

    @pl.loop(0, blocks)
    def key_block(i):
        chunk(kcodes_hbm, keys_ref, ksem, i).wait()
        first_page = i * PAGES
        slots = [
            outlier_ref[:, pl.ds(pl.multiple_of((first_page + p) * PAGE, PAGE), PAGE)].astype(F32)
            for p in range(PAGES)
        ]
        slots = jnp.concatenate(slots + [none] * (LANES // HEADS - PAGES), axis=0).T.astype(BF16)
        chosen = []
        for p in range(PAGES):
            column = [none] * (LANES // HEADS)
            column[p] = onehot[first_page + p]
            chosen.append(jnp.concatenate(column, axis=0).astype(BF16))
        correction = jnp.dot(slots, jnp.concatenate(chosen, axis=1), preferred_element_type=F32)
        for p in range(PAGES):
            rows = pl.ds(pl.multiple_of((first_page + p) * PAGE, PAGE), PAGE)
            base = keys_ref[rows, :].astype(F32) * kscale_ref[first_page + p]
            keys_ref[rows, :] = (base + correction[:, p * LANES : (p + 1) * LANES]).astype(BF16)

    @pl.loop(0, blocks)
    def value_block(i):
        chunk(vcodes_hbm, values_ref, vsem, i).wait()
        for p in range(PAGES):
            rows = pl.ds(pl.multiple_of((i * PAGES + p) * PAGE, PAGE), PAGE)
            values_ref[rows, :] = (
                values_ref[rows, :].astype(F32) * vscale_ref[i * PAGES + p]
            ).astype(BF16)


def attend_kernel(
    place_ref,
    q_ref,
    own_ref,
    keys_hbm,
    values_hbm,
    out_ref,
    keys_ref,
    values_ref,
    scores,
    peak,
    total,
    acc,
    ksem,
    sem,
):
    load = pltpu.make_async_copy(values_hbm, values_ref, sem)

    def chunk(i):
        rows = pl.ds(pl.multiple_of(i * BLOCK, BLOCK), BLOCK)
        return pltpu.make_async_copy(keys_hbm.at[rows, :], keys_ref.at[rows, :], ksem.at[i])

    for i in range(keys_ref.shape[0] // BLOCK):
        chunk(i).start()
    load.start()
    blocks = keys_ref.shape[0] // BLOCK
    queries = q_ref.shape[0]
    peak[...] = jnp.full(peak.shape, LOW, F32)

    @pl.loop(0, blocks)
    def score_block(i):
        chunk(i).wait()
        running = peak[...]
        for j in range(BLOCK // TILE):
            rows = pl.ds(pl.multiple_of(i * BLOCK + j * TILE, TILE), TILE)
            tile = nt(q_ref[...], keys_ref[rows, :])
            scores[i * (BLOCK // TILE) + j] = tile
            running = jnp.maximum(running, jnp.maximum(tile[:, :LANES], tile[:, LANES:]))
        peak[...] = running

    peak[...] = jnp.broadcast_to(
        jnp.max(peak[...], axis=1, keepdims=True) * SCORE_SCALE, peak.shape
    )
    total[...] = jnp.zeros(total.shape, F32)
    acc[...] = jnp.zeros(acc.shape, F32)
    load.wait()

    @pl.loop(0, blocks)
    def value_block(i):
        running = total[...]
        top = peak[...]
        weights = []
        for j in range(BLOCK // TILE):
            for p in range(TILE // PAGE):
                part = scores[i * (BLOCK // TILE) + j, :, p * LANES : (p + 1) * LANES]
                weight = jnp.exp2(part * SCORE_SCALE - top)
                running = running + weight
                weights.append(weight.astype(BF16))
        total[...] = running
        rows = pl.ds(pl.multiple_of(i * BLOCK, BLOCK), BLOCK)
        acc[...] += jnp.dot(
            jnp.concatenate(weights, axis=1), values_ref[rows, :], preferred_element_type=F32
        )

    total[...] = jnp.broadcast_to(jnp.sum(total[...], axis=1, keepdims=True), total.shape)

    own = pl.ds(pl.multiple_of(place_ref[0] * HEADS, HEADS), HEADS)
    top = jnp.maximum(peak[own, :], own_ref[0])
    fade, own_fade = jnp.exp2(peak[own, :] - top), jnp.exp2(own_ref[0] - top)
    peak[own, :] = top
    total[own, :] = total[own, :] * fade + own_ref[1] * own_fade
    acc[own, :] = acc[own, :] * fade + own_ref[2] * own_fade

    pieces = out_ref.shape[0]
    stride = queries // SPLIT * HEADS
    for c in range(pieces):
        rows = [
            slice(u * stride + c * HEADS, u * stride + (c + 1) * HEADS)
            for u in range(SPLIT // HEADS)
        ]
        part = [acc[r, :] / total[r, :] for r in rows]
        logs = [peak[r, :] + jnp.log2(total[r, :]) for r in rows]
        out_ref[c, :SPLIT, :] = jnp.concatenate(part, axis=0).astype(BF16)
        stat = split_rows(to_lanes(jnp.concatenate(logs, axis=0)))
        out_ref[c, SPLIT:, :] = jnp.broadcast_to(stat, (STATS, LANES))


def merge_kernel(in_ref, out_ref):
    sources = in_ref.shape[0]
    logs = [to_rows(in_ref[s, SPLIT:, :].astype(F32)[:1]) for s in range(sources)]
    top = functools.reduce(jnp.maximum, logs)
    sums = jnp.zeros(top.shape, F32)
    weighted = jnp.zeros((SPLIT, LANES), F32)
    for s in range(sources):
        weight = jnp.exp2(logs[s] - top)
        sums = sums + weight
        weighted = weighted + in_ref[s, :SPLIT, :].astype(F32) * weight
    merged = (weighted / sums).astype(BF16)
    copies, rows, lanes = out_ref.shape
    if rows > SPLIT:
        wide = jnp.broadcast_to(top + jnp.log2(sums), (SPLIT, LANES))
        stat = jnp.broadcast_to(split_rows(to_lanes(wide)), (STATS, LANES))
    for c in range(copies):
        out_ref[c, :SPLIT, :] = merged
        if rows > SPLIT:
            out_ref[c, SPLIT:, :] = stat


def project_kernel(in_ref, weight_ref, out_ref, wide):
    blocks = in_ref.shape[0]
    for c in range(blocks):
        block = in_ref[c].astype(F32)
        for u in range(SPLIT // HEADS):
            first = (u * blocks + c) * HEADS
            wide[first : first + HEADS, :] = block[u * HEADS : (u + 1) * HEADS]
    samples = blocks * SPLIT // HEADS
    result = jnp.zeros((samples, LANES), F32)
    for h in range(HEADS):
        part = wide[pl.ds(h, samples, stride=HEADS), :].astype(BF16)
        result = result + jnp.dot(
            part, weight_ref[h * LANES : (h + 1) * LANES, :], preferred_element_type=F32
        )
    out_ref[...] = result.astype(BF16)


def sum_kernel(in_ref, out_ref):
    result = in_ref[0].astype(F32)
    for c in range(1, in_ref.shape[0]):
        result = result + in_ref[c].astype(F32)
    out_ref[...] = result.astype(BF16)


def spread(block, axis):
    copies = jnp.broadcast_to(block[None], (lax.axis_size(axis),) + block.shape)
    return lax.all_to_all(copies, axis, 0, 0)


def prepare(
    queries,
    key_codes,
    key_scale,
    outlier_chan,
    outlier_val,
    value_codes,
    value_scale,
    suffix_keys,
    suffix_values,
    page_table,
    suffix_len,
):
    keys = key_codes.shape[0]
    pools = suffix_keys.shape[0]
    return pl.pallas_call(
        prepare_kernel,
        out_shape=(
            jax.ShapeDtypeStruct((keys, LANES), BF16),
            jax.ShapeDtypeStruct((keys, LANES), BF16),
            jax.ShapeDtypeStruct((3, HEADS, LANES), F32),
        ),
        in_specs=[HBM] * 11,
        out_specs=(VMEM, VMEM, VMEM),
        scratch_shapes=[
            pltpu.SMEM(suffix_len.shape, jnp.int32),
            pltpu.SMEM(page_table.shape, jnp.int32),
            pltpu.VMEM(queries.shape, BF16),
            pltpu.VMEM(key_scale.shape, F32),
            pltpu.VMEM((HEADS, keys // PAGE), jnp.int32),
            pltpu.VMEM((HEADS, keys), BF16),
            pltpu.VMEM(value_scale.shape, F32),
            pltpu.VMEM((pools, PAGE, LANES), BF16),
            pltpu.VMEM((pools, PAGE, LANES), BF16),
            pltpu.VMEM((keys // PAGE, HEADS, LANES), F32),
            pltpu.SemaphoreType.DMA((keys // BLOCK,)),
            pltpu.SemaphoreType.DMA((keys // BLOCK,)),
            pltpu.SemaphoreType.DMA((9,)),
        ],
        compiler_params=pltpu.CompilerParams(vmem_limit_bytes=PREPARE_LIMIT),
        cost_estimate=pl.CostEstimate(
            flops=2 * keys * LANES * LANES, bytes_accessed=10 * keys * LANES, transcendentals=0
        ),
        name="prepare",
    )(
        suffix_len,
        page_table,
        queries,
        key_scale,
        outlier_chan.reshape(-1, HEADS).T,
        outlier_val.reshape(-1, HEADS).T,
        value_scale,
        key_codes.reshape(keys, LANES),
        value_codes.reshape(keys, LANES),
        suffix_keys.reshape(pools, PAGE, LANES),
        suffix_values.reshape(pools, PAGE, LANES),
    )


def attend(place, all_queries, keys, values, own):
    rows = all_queries.shape[0]
    return pl.pallas_call(
        attend_kernel,
        out_shape=jax.ShapeDtypeStruct((rows // SPLIT, SPLIT + STATS, LANES), BF16),
        in_specs=[SMEM, VMEM, VMEM, HBM, HBM],
        out_specs=VMEM,
        scratch_shapes=[
            pltpu.VMEM(keys.shape, BF16),
            pltpu.VMEM(values.shape, BF16),
            pltpu.VMEM((keys.shape[0] // TILE, rows, TILE), F32),
            pltpu.VMEM((rows, LANES), F32),
            pltpu.VMEM((rows, LANES), F32),
            pltpu.VMEM((rows, LANES), F32),
            pltpu.SemaphoreType.DMA((keys.shape[0] // BLOCK,)),
            pltpu.SemaphoreType.DMA,
        ],
        compiler_params=pltpu.CompilerParams(vmem_limit_bytes=ATTEND_LIMIT),
        name="attend",
    )(place, all_queries, own, keys, values)


def shards(
    queries,
    key_codes,
    key_scale,
    outlier_chan,
    outlier_val,
    value_codes,
    value_scale,
    suffix_keys,
    suffix_values,
    page_table,
    suffix_len,
    out_weight,
):
    seq, near, far = ("zh", "zl", "y"), ("zl", "y"), "zh"
    samples = lax.axis_size(seq)
    queries = queries.reshape(HEADS, LANES)
    all_queries = spread(queries, seq).reshape(samples * HEADS, LANES)
    own = lax.axis_index(seq).astype(jnp.int32).reshape(1)
    params = pltpu.CompilerParams(vmem_limit_bytes=SMALL)
    prepared = prepare(
        queries,
        key_codes,
        key_scale,
        outlier_chan,
        outlier_val,
        value_codes,
        value_scale,
        suffix_keys,
        suffix_values,
        page_table,
        suffix_len,
    )
    partial = attend(own, all_queries, *prepared)
    partial = lax.all_to_all(partial, near, 0, 0)
    partial = pl.pallas_call(
        merge_kernel,
        out_shape=jax.ShapeDtypeStruct((lax.axis_size(far), SPLIT + STATS, LANES), BF16),
        in_specs=[VMEM],
        out_specs=VMEM,
        compiler_params=params,
        name="merge_near",
    )(partial)
    partial = lax.all_to_all(partial, far, 0, 0)
    attention = pl.pallas_call(
        merge_kernel,
        out_shape=jax.ShapeDtypeStruct((lax.axis_size(near), SPLIT, LANES), BF16),
        in_specs=[VMEM],
        out_specs=VMEM,
        compiler_params=params,
        name="merge_far",
    )(partial)
    attention = lax.all_to_all(attention, near, 0, 0)
    product = pl.pallas_call(
        project_kernel,
        out_shape=jax.ShapeDtypeStruct((samples, LANES), BF16),
        in_specs=[VMEM, VMEM],
        out_specs=VMEM,
        scratch_shapes=[pltpu.VMEM((samples * HEADS, LANES), F32)],
        compiler_params=params,
        name="project",
    )(attention, out_weight)
    tp = lax.axis_size("x") * lax.axis_size("core")
    product = lax.all_to_all(product.reshape(tp, samples // tp, LANES), ("x", "core"), 0, 0)
    return pl.pallas_call(
        sum_kernel,
        out_shape=jax.ShapeDtypeStruct((samples // tp, LANES), BF16),
        in_specs=[VMEM],
        out_specs=VMEM,
        compiler_params=params,
        name="sum_tp",
    )(product)


def solution(mesh):
    grid = Mesh(mesh.devices.reshape(4, 4, 4, 4, 2), ("zh", "zl", "y", "x", "core"))
    seq, tp = ("zh", "zl", "y"), ("x", "core")
    return jax.shard_map(
        shards,
        mesh=grid,
        in_specs=(
            P(seq, tp, None),
            P(seq, tp, None),
            P(seq, tp, None),
            P(seq, tp, None),
            P(seq, tp, None),
            P(seq, tp, None),
            P(seq, tp, None),
            P(seq, None, tp, None),
            P(seq, None, tp, None),
            P(seq, None),
            P(seq),
            P(tp, seq),
        ),
        out_specs=P(tp, seq),
        check_vma=False,
    )
```

```python
import functools
import math

import jax
import jax.numpy as jnp
from jax import lax
from jax.experimental import pallas as pl
from jax.experimental.pallas import tpu as pltpu
from jax.sharding import Mesh, PartitionSpec as P

F32 = jnp.float32
BF16 = jnp.bfloat16
LANES = 128
HEADS = 8
PAGE = 128
TILE = 256
BLOCK = 1024
ROOM = 256
PAGES = BLOCK // PAGE
SCORE_SCALE = math.log2(math.e) / math.sqrt(LANES)
SPLIT = 32
STATS = 16
LOW = -1e30
VMEM = pl.BlockSpec(memory_space=pltpu.VMEM)
SMEM = pl.BlockSpec(memory_space=pltpu.SMEM)
HBM = pl.BlockSpec(memory_space=pltpu.HBM)
PREPARE_LIMIT = 54 * 1024 * 1024
ATTEND_LIMIT = 53 * 1024 * 1024
SMALL = 4 * 1024 * 1024


def nt(a, b):
    return lax.dot_general(a, b, (((1,), (1,)), ((), ())), preferred_element_type=F32)


def split_rows(row):
    high = row.astype(BF16).astype(F32)
    rest = row - high
    middle = rest.astype(BF16).astype(F32)
    low = rest - middle
    part = lax.broadcasted_iota(jnp.int32, row.shape, row.ndim - 1) // SPLIT
    kept = jnp.where(part == 0, high, jnp.where(part == 1, middle, low))
    return jnp.where(part < 3, kept, 0.0).astype(BF16)


def to_lanes(columns):
    row = lax.broadcasted_iota(jnp.int32, columns.shape, 0)
    lane = lax.broadcasted_iota(jnp.int32, columns.shape, 1)
    return jnp.sum(jnp.where(lane % SPLIT == row, columns, 0.0), axis=0, keepdims=True)


def to_rows(stat):
    wide = jnp.broadcast_to(stat, (SPLIT, LANES))
    row = lax.broadcasted_iota(jnp.int32, wide.shape, 0)
    lane = lax.broadcasted_iota(jnp.int32, wide.shape, 1)
    return jnp.sum(jnp.where(lane % SPLIT == row, wide, 0.0), axis=1, keepdims=True)


def prepare_kernel(
    len_hbm,
    table_hbm,
    own_q_hbm,
    kscale_hbm,
    chan_hbm,
    outlier_hbm,
    vscale_hbm,
    kcodes_hbm,
    vcodes_hbm,
    skeys_hbm,
    svalues_hbm,
    keys_hbm,
    values_hbm,
    own_hbm,
    len_ref,
    table_ref,
    own_q_ref,
    kscale_ref,
    chan_ref,
    outlier_ref,
    vscale_ref,
    skbuf,
    svbuf,
    kbuf,
    vbuf,
    own_ref,
    onehot,
    ksem,
    vsem,
    kout,
    vout,
    sem,
):
    blocks = kbuf.shape[0] // BLOCK

    def block_rows(i):
        return pl.ds(pl.multiple_of(i * BLOCK, BLOCK), BLOCK)

    def chunk(hbm, buf, sems, i):
        return pltpu.make_async_copy(hbm.at[block_rows(i), :], buf.at[block_rows(i), :], sems.at[i])

    small = [
        pltpu.make_async_copy(source, target, sem.at[n])
        for n, (source, target) in enumerate(
            (
                (chan_hbm, chan_ref),
                (outlier_hbm, outlier_ref),
                (kscale_hbm, kscale_ref),
                (vscale_hbm, vscale_ref),
                (own_q_hbm, own_q_ref),
                (skeys_hbm, skbuf),
                (svalues_hbm, svbuf),
                (len_hbm, len_ref),
                (table_hbm, table_ref),
            )
        )
    ]
    result = pltpu.make_async_copy(own_ref, own_hbm.at[0], sem.at[len(small)])
    for copy in small[:3]:
        copy.start()
    for i in range(blocks):
        chunk(kcodes_hbm, kbuf, ksem, i).start()
    for copy in small[3:]:
        copy.start()
    for i in range(blocks):
        chunk(vcodes_hbm, vbuf, vsem, i).start()
    small[0].wait()

    lane = lax.broadcasted_iota(jnp.int32, (HEADS, LANES), 1)
    channels = chan_ref[...]
    for page in range(onehot.shape[0]):
        onehot[page] = (lane == channels[:, page : page + 1]).astype(F32)
    none = jnp.zeros((HEADS, LANES), F32)
    for copy in small[1:3]:
        copy.wait()

    @pl.loop(0, blocks)
    def key_block(i):
        chunk(kcodes_hbm, kbuf, ksem, i).wait()
        first_page = i * PAGES
        slots = [
            outlier_ref[:, pl.ds(pl.multiple_of((first_page + p) * PAGE, PAGE), PAGE)].astype(F32)
            for p in range(PAGES)
        ]
        slots = jnp.concatenate(slots + [none] * (LANES // HEADS - PAGES), axis=0).T.astype(BF16)
        chosen = []
        for p in range(PAGES):
            column = [none] * (LANES // HEADS)
            column[p] = onehot[first_page + p]
            chosen.append(jnp.concatenate(column, axis=0).astype(BF16))
        correction = jnp.dot(slots, jnp.concatenate(chosen, axis=1), preferred_element_type=F32)
        for p in range(PAGES):
            rows = pl.ds(pl.multiple_of((first_page + p) * PAGE, PAGE), PAGE)
            base = kbuf[rows, :].astype(F32) * kscale_ref[first_page + p]
            kbuf[rows, :] = (base + correction[:, p * LANES : (p + 1) * LANES]).astype(BF16)
        pltpu.make_async_copy(
            kbuf.at[block_rows(i), :], keys_hbm.at[block_rows(i), :], kout.at[i]
        ).start()

    for copy in small[3:]:
        copy.wait()
    live = len_ref[0]
    own_scores = [
        jnp.where(
            lane + j * PAGE < live,
            nt(own_q_ref[...], skbuf[table_ref[0, j]]) * SCORE_SCALE,
            LOW,
        )
        for j in range(skbuf.shape[0])
    ]
    top = functools.reduce(jnp.maximum, own_scores)
    top = jnp.max(top, axis=1, keepdims=True)
    sums = jnp.zeros((HEADS, LANES), F32)
    weighted = jnp.zeros((HEADS, LANES), F32)
    for j, part in enumerate(own_scores):
        weight = jnp.where(lane + j * PAGE < live, jnp.exp2(part - top), 0.0)
        sums = sums + weight
        weighted = weighted + jnp.dot(
            weight.astype(BF16), svbuf[table_ref[0, j]], preferred_element_type=F32
        )
    own_ref[0] = jnp.broadcast_to(top, (HEADS, LANES))
    own_ref[1] = jnp.broadcast_to(jnp.sum(sums, axis=1, keepdims=True), (HEADS, LANES))
    own_ref[2] = weighted
    result.start()

    @pl.loop(0, blocks)
    def value_block(i):
        chunk(vcodes_hbm, vbuf, vsem, i).wait()
        for p in range(PAGES):
            rows = pl.ds(pl.multiple_of((i * PAGES + p) * PAGE, PAGE), PAGE)
            vbuf[rows, :] = (vbuf[rows, :].astype(F32) * vscale_ref[i * PAGES + p]).astype(BF16)
        pltpu.make_async_copy(
            vbuf.at[block_rows(i), :], values_hbm.at[block_rows(i), :], vout.at[i]
        ).start()

    for i in range(blocks):
        pltpu.make_async_copy(
            kbuf.at[block_rows(i), :], keys_hbm.at[block_rows(i), :], kout.at[i]
        ).wait()
        pltpu.make_async_copy(
            vbuf.at[block_rows(i), :], values_hbm.at[block_rows(i), :], vout.at[i]
        ).wait()
    result.wait()


def attend_kernel(
    place_ref,
    q_ref,
    own_hbm,
    keys_hbm,
    values_hbm,
    out_ref,
    own_ref,
    keys_ref,
    values_ref,
    scores,
    peak,
    total,
    acc,
    ksem,
    sem,
):
    load = pltpu.make_async_copy(values_hbm, values_ref, sem.at[0])
    own_load = pltpu.make_async_copy(own_hbm.at[0], own_ref, sem.at[1])

    def chunk(i):
        rows = pl.ds(pl.multiple_of(i * BLOCK, BLOCK), BLOCK)
        return pltpu.make_async_copy(keys_hbm.at[rows, :], keys_ref.at[rows, :], ksem.at[i])

    for i in range(keys_ref.shape[0] // BLOCK):
        chunk(i).start()
    load.start()
    own_load.start()
    blocks = keys_ref.shape[0] // BLOCK
    queries = q_ref.shape[0]
    peak[...] = jnp.full(peak.shape, LOW, F32)

    @pl.loop(0, blocks)
    def score_block(i):
        chunk(i).wait()
        running = peak[...]
        for j in range(BLOCK // TILE):
            rows = pl.ds(pl.multiple_of(i * BLOCK + j * TILE, TILE), TILE)
            tile = nt(q_ref[...], keys_ref[rows, :])
            scores[i * (BLOCK // TILE) + j] = tile
            running = jnp.maximum(running, jnp.maximum(tile[:, :LANES], tile[:, LANES:]))
        peak[...] = running

    peak[...] = jnp.broadcast_to(
        jnp.max(peak[...], axis=1, keepdims=True) * SCORE_SCALE, peak.shape
    )
    total[...] = jnp.zeros(total.shape, F32)
    acc[...] = jnp.zeros(acc.shape, F32)
    load.wait()
    own_load.wait()

    @pl.loop(0, blocks, unroll=True)
    def value_block(i):
        running = total[...]
        top = peak[...]
        weights = []
        for j in range(BLOCK // TILE):
            for p in range(TILE // PAGE):
                part = scores[i * (BLOCK // TILE) + j, :, p * LANES : (p + 1) * LANES]
                weight = jnp.exp2(part * SCORE_SCALE - top)
                running = running + weight
                weights.append(weight.astype(BF16))
        total[...] = running
        rows = pl.ds(pl.multiple_of(i * BLOCK, BLOCK), BLOCK)
        acc[...] += jnp.dot(
            jnp.concatenate(weights, axis=1), values_ref[rows, :], preferred_element_type=F32
        )

    total[...] = jnp.broadcast_to(jnp.sum(total[...], axis=1, keepdims=True), total.shape)

    own = pl.ds(pl.multiple_of(place_ref[0] * HEADS, HEADS), HEADS)
    top = jnp.maximum(peak[own, :], own_ref[0])
    fade, own_fade = jnp.exp2(peak[own, :] - top), jnp.exp2(own_ref[0] - top)
    peak[own, :] = top
    total[own, :] = total[own, :] * fade + own_ref[1] * own_fade
    acc[own, :] = acc[own, :] * fade + own_ref[2] * own_fade

    pieces = out_ref.shape[0]
    stride = queries // SPLIT * HEADS
    for c in range(pieces):
        rows = [
            slice(u * stride + c * HEADS, u * stride + (c + 1) * HEADS)
            for u in range(SPLIT // HEADS)
        ]
        part = [acc[r, :] / total[r, :] for r in rows]
        logs = [peak[r, :] + jnp.log2(total[r, :]) for r in rows]
        out_ref[c, :SPLIT, :] = jnp.concatenate(part, axis=0).astype(BF16)
        stat = split_rows(to_lanes(jnp.concatenate(logs, axis=0)))
        out_ref[c, SPLIT:, :] = jnp.broadcast_to(stat, (STATS, LANES))


def merge_kernel(in_ref, out_ref):
    sources = in_ref.shape[0]
    logs = [to_rows(in_ref[s, SPLIT:, :].astype(F32)[:1]) for s in range(sources)]
    top = functools.reduce(jnp.maximum, logs)
    sums = jnp.zeros(top.shape, F32)
    weighted = jnp.zeros((SPLIT, LANES), F32)
    for s in range(sources):
        weight = jnp.exp2(logs[s] - top)
        sums = sums + weight
        weighted = weighted + in_ref[s, :SPLIT, :].astype(F32) * weight
    merged = (weighted / sums).astype(BF16)
    copies, rows, lanes = out_ref.shape
    if rows > SPLIT:
        wide = jnp.broadcast_to(top + jnp.log2(sums), (SPLIT, LANES))
        stat = jnp.broadcast_to(split_rows(to_lanes(wide)), (STATS, LANES))
    for c in range(copies):
        out_ref[c, :SPLIT, :] = merged
        if rows > SPLIT:
            out_ref[c, SPLIT:, :] = stat


def project_kernel(in_ref, weight_ref, out_ref, wide):
    blocks = in_ref.shape[0]
    for c in range(blocks):
        block = in_ref[c].astype(F32)
        for u in range(SPLIT // HEADS):
            first = (u * blocks + c) * HEADS
            wide[first : first + HEADS, :] = block[u * HEADS : (u + 1) * HEADS]
    samples = blocks * SPLIT // HEADS
    result = jnp.zeros((samples, LANES), F32)
    for h in range(HEADS):
        part = wide[pl.ds(h, samples, stride=HEADS), :].astype(BF16)
        result = result + jnp.dot(
            part, weight_ref[h * LANES : (h + 1) * LANES, :], preferred_element_type=F32
        )
    out_ref[...] = result.astype(BF16)


def sum_kernel(in_ref, out_ref):
    result = in_ref[0].astype(F32)
    for c in range(1, in_ref.shape[0]):
        result = result + in_ref[c].astype(F32)
    out_ref[...] = result.astype(BF16)


def spread(block, axis):
    copies = jnp.broadcast_to(block[None], (lax.axis_size(axis),) + block.shape)
    return lax.all_to_all(copies, axis, 0, 0)


def prepare(
    queries,
    key_codes,
    key_scale,
    outlier_chan,
    outlier_val,
    value_codes,
    value_scale,
    suffix_keys,
    suffix_values,
    page_table,
    suffix_len,
):
    keys = key_codes.shape[0]
    pools = suffix_keys.shape[0]
    return pl.pallas_call(
        prepare_kernel,
        out_shape=(
            jax.ShapeDtypeStruct((keys, LANES), BF16),
            jax.ShapeDtypeStruct((keys, LANES), BF16),
            jax.ShapeDtypeStruct((ROOM, 3, HEADS, LANES), F32),
        ),
        in_specs=[HBM] * 11,
        out_specs=(HBM, HBM, HBM),
        scratch_shapes=[
            pltpu.SMEM(suffix_len.shape, jnp.int32),
            pltpu.SMEM(page_table.shape, jnp.int32),
            pltpu.VMEM(queries.shape, BF16),
            pltpu.VMEM(key_scale.shape, F32),
            pltpu.VMEM((HEADS, keys // PAGE), jnp.int32),
            pltpu.VMEM((HEADS, keys), BF16),
            pltpu.VMEM(value_scale.shape, F32),
            pltpu.VMEM((pools, PAGE, LANES), BF16),
            pltpu.VMEM((pools, PAGE, LANES), BF16),
            pltpu.VMEM((keys, LANES), BF16),
            pltpu.VMEM((keys, LANES), BF16),
            pltpu.VMEM((3, HEADS, LANES), F32),
            pltpu.VMEM((keys // PAGE, HEADS, LANES), F32),
            pltpu.SemaphoreType.DMA((keys // BLOCK,)),
            pltpu.SemaphoreType.DMA((keys // BLOCK,)),
            pltpu.SemaphoreType.DMA((keys // BLOCK,)),
            pltpu.SemaphoreType.DMA((keys // BLOCK,)),
            pltpu.SemaphoreType.DMA((10,)),
        ],
        compiler_params=pltpu.CompilerParams(vmem_limit_bytes=PREPARE_LIMIT),
        cost_estimate=pl.CostEstimate(
            flops=2 * keys * LANES * LANES, bytes_accessed=10 * keys * LANES, transcendentals=0
        ),
        name="prepare",
    )(
        suffix_len,
        page_table,
        queries,
        key_scale,
        outlier_chan.reshape(-1, HEADS).T,
        outlier_val.reshape(-1, HEADS).T,
        value_scale,
        key_codes.reshape(keys, LANES),
        value_codes.reshape(keys, LANES),
        suffix_keys.reshape(pools, PAGE, LANES),
        suffix_values.reshape(pools, PAGE, LANES),
    )


def attend(place, all_queries, keys, values, own):
    rows = all_queries.shape[0]
    return pl.pallas_call(
        attend_kernel,
        out_shape=jax.ShapeDtypeStruct((rows // SPLIT, SPLIT + STATS, LANES), BF16),
        in_specs=[SMEM, VMEM, HBM, HBM, HBM],
        out_specs=VMEM,
        scratch_shapes=[
            pltpu.VMEM(own.shape[1:], F32),
            pltpu.VMEM(keys.shape, BF16),
            pltpu.VMEM(values.shape, BF16),
            pltpu.VMEM((keys.shape[0] // TILE, rows, TILE), F32),
            pltpu.VMEM((rows, LANES), F32),
            pltpu.VMEM((rows, LANES), F32),
            pltpu.VMEM((rows, LANES), F32),
            pltpu.SemaphoreType.DMA((keys.shape[0] // BLOCK,)),
            pltpu.SemaphoreType.DMA((2,)),
        ],
        compiler_params=pltpu.CompilerParams(vmem_limit_bytes=ATTEND_LIMIT),
        name="attend",
    )(place, all_queries, own, keys, values)


def shards(
    queries,
    key_codes,
    key_scale,
    outlier_chan,
    outlier_val,
    value_codes,
    value_scale,
    suffix_keys,
    suffix_values,
    page_table,
    suffix_len,
    out_weight,
):
    seq, near, far = ("zh", "zl", "y"), ("zl", "y"), "zh"
    samples = lax.axis_size(seq)
    queries = queries.reshape(HEADS, LANES)
    all_queries = spread(queries, seq).reshape(samples * HEADS, LANES)
    own = lax.axis_index(seq).astype(jnp.int32).reshape(1)
    params = pltpu.CompilerParams(vmem_limit_bytes=SMALL)
    prepared = prepare(
        queries,
        key_codes,
        key_scale,
        outlier_chan,
        outlier_val,
        value_codes,
        value_scale,
        suffix_keys,
        suffix_values,
        page_table,
        suffix_len,
    )
    partial = attend(own, all_queries, *prepared)
    partial = lax.all_to_all(partial, near, 0, 0)
    partial = pl.pallas_call(
        merge_kernel,
        out_shape=jax.ShapeDtypeStruct((lax.axis_size(far), SPLIT + STATS, LANES), BF16),
        in_specs=[VMEM],
        out_specs=VMEM,
        compiler_params=params,
        name="merge_near",
    )(partial)
    partial = lax.all_to_all(partial, far, 0, 0)
    attention = pl.pallas_call(
        merge_kernel,
        out_shape=jax.ShapeDtypeStruct((lax.axis_size(near), SPLIT, LANES), BF16),
        in_specs=[VMEM],
        out_specs=VMEM,
        compiler_params=params,
        name="merge_far",
    )(partial)
    attention = lax.all_to_all(attention, near, 0, 0)
    product = pl.pallas_call(
        project_kernel,
        out_shape=jax.ShapeDtypeStruct((samples, LANES), BF16),
        in_specs=[VMEM, VMEM],
        out_specs=VMEM,
        scratch_shapes=[pltpu.VMEM((samples * HEADS, LANES), F32)],
        compiler_params=params,
        name="project",
    )(attention, out_weight)
    tp = lax.axis_size("x") * lax.axis_size("core")
    product = lax.all_to_all(product.reshape(tp, samples // tp, LANES), ("x", "core"), 0, 0)
    return pl.pallas_call(
        sum_kernel,
        out_shape=jax.ShapeDtypeStruct((samples // tp, LANES), BF16),
        in_specs=[VMEM],
        out_specs=VMEM,
        compiler_params=params,
        name="sum_tp",
    )(product)


def solution(mesh):
    grid = Mesh(mesh.devices.reshape(4, 4, 4, 4, 2), ("zh", "zl", "y", "x", "core"))
    seq, tp = ("zh", "zl", "y"), ("x", "core")
    return jax.shard_map(
        shards,
        mesh=grid,
        in_specs=(
            P(seq, tp, None),
            P(seq, tp, None),
            P(seq, tp, None),
            P(seq, tp, None),
            P(seq, tp, None),
            P(seq, tp, None),
            P(seq, tp, None),
            P(seq, None, tp, None),
            P(seq, None, tp, None),
            P(seq, None),
            P(seq),
            P(tp, seq),
        ),
        out_specs=P(tp, seq),
        check_vma=False,
    )
```

```python
import functools
import math

import jax
import jax.numpy as jnp
from jax import lax
from jax.experimental import pallas as pl
from jax.experimental.pallas import tpu as pltpu
from jax.sharding import Mesh, PartitionSpec as P

F32 = jnp.float32
BF16 = jnp.bfloat16
LANES = 128
HEADS = 8
PAGE = 128
TILE = 256
BLOCK = 1024
ROOM = 256
PAGES = BLOCK // PAGE
SCORE_SCALE = math.log2(math.e) / math.sqrt(LANES)
SPLIT = 32
GROUP = 64
STATS = 16
LOW = -1e30
VMEM = pl.BlockSpec(memory_space=pltpu.VMEM)
SMEM = pl.BlockSpec(memory_space=pltpu.SMEM)
HBM = pl.BlockSpec(memory_space=pltpu.HBM)
PREPARE_LIMIT = 54 * 1024 * 1024
ATTEND_LIMIT = 53 * 1024 * 1024
SMALL = 4 * 1024 * 1024


def nt(a, b):
    return lax.dot_general(a, b, (((1,), (1,)), ((), ())), preferred_element_type=F32)


def split_rows(row):
    high = row.astype(BF16).astype(F32)
    rest = row - high
    middle = rest.astype(BF16).astype(F32)
    low = rest - middle
    part = lax.broadcasted_iota(jnp.int32, row.shape, row.ndim - 1) // SPLIT
    kept = jnp.where(part == 0, high, jnp.where(part == 1, middle, low))
    return jnp.where(part < 3, kept, 0.0).astype(BF16)


def to_lanes(columns):
    row = lax.broadcasted_iota(jnp.int32, columns.shape, 0)
    lane = lax.broadcasted_iota(jnp.int32, columns.shape, 1)
    return jnp.sum(jnp.where(lane % SPLIT == row, columns, 0.0), axis=0, keepdims=True)


def stat_rows(logs):
    copies = STATS * SPLIT // GROUP
    rows = [
        jnp.broadcast_to(to_lanes(logs[at : at + SPLIT]), (copies, LANES))
        for at in range(0, GROUP, SPLIT)
    ]
    return split_rows(jnp.concatenate(rows, axis=0))


def to_rows(stat):
    wide = jnp.broadcast_to(stat, (SPLIT, LANES))
    row = lax.broadcasted_iota(jnp.int32, wide.shape, 0)
    lane = lax.broadcasted_iota(jnp.int32, wide.shape, 1)
    return jnp.sum(jnp.where(lane % SPLIT == row, wide, 0.0), axis=1, keepdims=True)


def prepare_kernel(
    len_hbm,
    table_hbm,
    own_q_hbm,
    kscale_hbm,
    chan_hbm,
    outlier_hbm,
    vscale_hbm,
    kcodes_hbm,
    vcodes_hbm,
    skeys_hbm,
    svalues_hbm,
    keys_hbm,
    values_hbm,
    own_hbm,
    len_ref,
    table_ref,
    own_q_ref,
    kscale_ref,
    chan_ref,
    outlier_ref,
    vscale_ref,
    skbuf,
    svbuf,
    kbuf,
    vbuf,
    own_ref,
    onehot,
    ksem,
    vsem,
    kout,
    vout,
    sem,
):
    blocks = kbuf.shape[0] // BLOCK

    def block_rows(i):
        return pl.ds(pl.multiple_of(i * BLOCK, BLOCK), BLOCK)

    def chunk(hbm, buf, sems, i):
        return pltpu.make_async_copy(hbm.at[block_rows(i), :], buf.at[block_rows(i), :], sems.at[i])

    small = [
        pltpu.make_async_copy(source, target, sem.at[n])
        for n, (source, target) in enumerate(
            (
                (chan_hbm, chan_ref),
                (outlier_hbm, outlier_ref),
                (kscale_hbm, kscale_ref),
                (vscale_hbm, vscale_ref),
                (own_q_hbm, own_q_ref),
                (skeys_hbm, skbuf),
                (svalues_hbm, svbuf),
                (len_hbm, len_ref),
                (table_hbm, table_ref),
            )
        )
    ]
    result = pltpu.make_async_copy(own_ref, own_hbm.at[0], sem.at[len(small)])
    for copy in small[:3]:
        copy.start()
    for i in range(blocks):
        chunk(kcodes_hbm, kbuf, ksem, i).start()
    for copy in small[3:]:
        copy.start()
    for i in range(blocks):
        chunk(vcodes_hbm, vbuf, vsem, i).start()
    small[0].wait()

    lane = lax.broadcasted_iota(jnp.int32, (HEADS, LANES), 1)
    channels = chan_ref[...]
    for page in range(onehot.shape[0]):
        onehot[page] = (lane == channels[:, page : page + 1]).astype(F32)
    none = jnp.zeros((HEADS, LANES), F32)
    for copy in small[1:3]:
        copy.wait()

    @pl.loop(0, blocks)
    def key_block(i):
        chunk(kcodes_hbm, kbuf, ksem, i).wait()
        first_page = i * PAGES
        slots = [
            outlier_ref[:, pl.ds(pl.multiple_of((first_page + p) * PAGE, PAGE), PAGE)].astype(F32)
            for p in range(PAGES)
        ]
        slots = jnp.concatenate(slots + [none] * (LANES // HEADS - PAGES), axis=0).T.astype(BF16)
        chosen = []
        for p in range(PAGES):
            column = [none] * (LANES // HEADS)
            column[p] = onehot[first_page + p]
            chosen.append(jnp.concatenate(column, axis=0).astype(BF16))
        correction = jnp.dot(slots, jnp.concatenate(chosen, axis=1), preferred_element_type=F32)
        for p in range(PAGES):
            rows = pl.ds(pl.multiple_of((first_page + p) * PAGE, PAGE), PAGE)
            base = kbuf[rows, :].astype(F32) * kscale_ref[first_page + p]
            kbuf[rows, :] = (base + correction[:, p * LANES : (p + 1) * LANES]).astype(BF16)
        pltpu.make_async_copy(
            kbuf.at[block_rows(i), :], keys_hbm.at[block_rows(i), :], kout.at[i]
        ).start()

    for copy in small[3:]:
        copy.wait()
    live = len_ref[0]
    own_scores = [
        jnp.where(
            lane + j * PAGE < live,
            nt(own_q_ref[...], skbuf[table_ref[0, j]]) * SCORE_SCALE,
            LOW,
        )
        for j in range(skbuf.shape[0])
    ]
    top = functools.reduce(jnp.maximum, own_scores)
    top = jnp.max(top, axis=1, keepdims=True)
    sums = jnp.zeros((HEADS, LANES), F32)
    weighted = jnp.zeros((HEADS, LANES), F32)
    for j, part in enumerate(own_scores):
        weight = jnp.where(lane + j * PAGE < live, jnp.exp2(part - top), 0.0)
        sums = sums + weight
        weighted = weighted + jnp.dot(
            weight.astype(BF16), svbuf[table_ref[0, j]], preferred_element_type=F32
        )
    own_ref[0] = jnp.broadcast_to(top, (HEADS, LANES))
    own_ref[1] = jnp.broadcast_to(jnp.sum(sums, axis=1, keepdims=True), (HEADS, LANES))
    own_ref[2] = weighted
    result.start()

    @pl.loop(0, blocks)
    def value_block(i):
        chunk(vcodes_hbm, vbuf, vsem, i).wait()
        for p in range(PAGES):
            rows = pl.ds(pl.multiple_of((i * PAGES + p) * PAGE, PAGE), PAGE)
            vbuf[rows, :] = (vbuf[rows, :].astype(F32) * vscale_ref[i * PAGES + p]).astype(BF16)
        pltpu.make_async_copy(
            vbuf.at[block_rows(i), :], values_hbm.at[block_rows(i), :], vout.at[i]
        ).start()

    for i in range(blocks):
        pltpu.make_async_copy(
            kbuf.at[block_rows(i), :], keys_hbm.at[block_rows(i), :], kout.at[i]
        ).wait()
        pltpu.make_async_copy(
            vbuf.at[block_rows(i), :], values_hbm.at[block_rows(i), :], vout.at[i]
        ).wait()
    result.wait()


def attend_kernel(
    place_ref,
    q_ref,
    own_hbm,
    keys_hbm,
    values_hbm,
    out_ref,
    own_ref,
    keys_ref,
    values_ref,
    scores,
    peak,
    total,
    acc,
    ksem,
    sem,
):
    load = pltpu.make_async_copy(values_hbm, values_ref, sem.at[0])
    own_load = pltpu.make_async_copy(own_hbm.at[0], own_ref, sem.at[1])

    def chunk(i):
        rows = pl.ds(pl.multiple_of(i * BLOCK, BLOCK), BLOCK)
        return pltpu.make_async_copy(keys_hbm.at[rows, :], keys_ref.at[rows, :], ksem.at[i])

    for i in range(keys_ref.shape[0] // BLOCK):
        chunk(i).start()
    load.start()
    own_load.start()
    blocks = keys_ref.shape[0] // BLOCK
    queries = q_ref.shape[0]
    peak[...] = jnp.full(peak.shape, LOW, F32)

    @pl.loop(0, blocks)
    def score_block(i):
        chunk(i).wait()
        running = peak[...]
        for j in range(BLOCK // TILE):
            rows = pl.ds(pl.multiple_of(i * BLOCK + j * TILE, TILE), TILE)
            tile = nt(q_ref[...], keys_ref[rows, :])
            scores[i * (BLOCK // TILE) + j] = tile
            running = jnp.maximum(running, jnp.maximum(tile[:, :LANES], tile[:, LANES:]))
        peak[...] = running

    peak[...] = jnp.broadcast_to(
        jnp.max(peak[...], axis=1, keepdims=True) * SCORE_SCALE, peak.shape
    )
    total[...] = jnp.zeros(total.shape, F32)
    acc[...] = jnp.zeros(acc.shape, F32)
    load.wait()
    own_load.wait()

    @pl.loop(0, blocks, unroll=True)
    def value_block(i):
        running = total[...]
        top = peak[...]
        weights = []
        for j in range(BLOCK // TILE):
            for p in range(TILE // PAGE):
                part = scores[i * (BLOCK // TILE) + j, :, p * LANES : (p + 1) * LANES]
                weight = jnp.exp2(part * SCORE_SCALE - top)
                running = running + weight
                weights.append(weight.astype(BF16))
        total[...] = running
        rows = pl.ds(pl.multiple_of(i * BLOCK, BLOCK), BLOCK)
        acc[...] += jnp.dot(
            jnp.concatenate(weights, axis=1), values_ref[rows, :], preferred_element_type=F32
        )

    total[...] = jnp.broadcast_to(jnp.sum(total[...], axis=1, keepdims=True), total.shape)

    own = pl.ds(pl.multiple_of(place_ref[0] * HEADS, HEADS), HEADS)
    top = jnp.maximum(peak[own, :], own_ref[0])
    fade, own_fade = jnp.exp2(peak[own, :] - top), jnp.exp2(own_ref[0] - top)
    peak[own, :] = top
    total[own, :] = total[own, :] * fade + own_ref[1] * own_fade
    acc[own, :] = acc[own, :] * fade + own_ref[2] * own_fade

    pieces = out_ref.shape[0]
    for c in range(pieces):
        rows = [
            slice((u * pieces + c) * HEADS, (u * pieces + c + 1) * HEADS)
            for u in range(GROUP // HEADS)
        ]
        part = [acc[r, :] / total[r, :] for r in rows]
        logs = [peak[r, :] + jnp.log2(total[r, :]) for r in rows]
        out_ref[c, :GROUP, :] = jnp.concatenate(part, axis=0).astype(BF16)
        out_ref[c, GROUP:, :] = stat_rows(jnp.concatenate(logs, axis=0))


def merge_kernel(in_ref, out_ref):
    sources = in_ref.shape[0]
    logs = []
    for s in range(sources):
        stats = in_ref[s, GROUP:, :].astype(F32)
        first = [at * STATS // GROUP for at in range(0, GROUP, SPLIT)]
        logs.append(jnp.concatenate([to_rows(stats[at : at + 1]) for at in first], axis=0))
    top = functools.reduce(jnp.maximum, logs)
    sums = jnp.zeros(top.shape, F32)
    weighted = jnp.zeros((GROUP, LANES), F32)
    for s in range(sources):
        weight = jnp.exp2(logs[s] - top)
        sums = sums + weight
        weighted = weighted + in_ref[s, :GROUP, :].astype(F32) * weight
    merged = (weighted / sums).astype(BF16)
    copies, rows, lanes = out_ref.shape
    if rows > GROUP:
        stat = stat_rows(jnp.broadcast_to(top + jnp.log2(sums), (GROUP, LANES)))
    for c in range(copies):
        out_ref[c, :GROUP, :] = merged
        if rows > GROUP:
            out_ref[c, GROUP:, :] = stat


def project_kernel(in_ref, weight_ref, out_ref, wide):
    blocks = in_ref.shape[0]
    for c in range(blocks):
        block = in_ref[c].astype(F32)
        for u in range(GROUP // HEADS):
            first = (u * blocks + c) * HEADS
            wide[first : first + HEADS, :] = block[u * HEADS : (u + 1) * HEADS]
    samples = blocks * GROUP // HEADS
    result = jnp.zeros((samples, LANES), F32)
    for h in range(HEADS):
        part = wide[pl.ds(h, samples, stride=HEADS), :].astype(BF16)
        result = result + jnp.dot(
            part, weight_ref[h * LANES : (h + 1) * LANES, :], preferred_element_type=F32
        )
    out_ref[...] = result.astype(BF16)


def sum_kernel(in_ref, out_ref):
    result = in_ref[0].astype(F32)
    for c in range(1, in_ref.shape[0]):
        result = result + in_ref[c].astype(F32)
    out_ref[...] = result.astype(BF16)


def spread(block, axis):
    copies = jnp.broadcast_to(block[None], (lax.axis_size(axis),) + block.shape)
    return lax.all_to_all(copies, axis, 0, 0)


def prepare(
    queries,
    key_codes,
    key_scale,
    outlier_chan,
    outlier_val,
    value_codes,
    value_scale,
    suffix_keys,
    suffix_values,
    page_table,
    suffix_len,
):
    keys = key_codes.shape[0]
    pools = suffix_keys.shape[0]
    return pl.pallas_call(
        prepare_kernel,
        out_shape=(
            jax.ShapeDtypeStruct((keys, LANES), BF16),
            jax.ShapeDtypeStruct((keys, LANES), BF16),
            jax.ShapeDtypeStruct((ROOM, 3, HEADS, LANES), F32),
        ),
        in_specs=[HBM] * 11,
        out_specs=(HBM, HBM, HBM),
        scratch_shapes=[
            pltpu.SMEM(suffix_len.shape, jnp.int32),
            pltpu.SMEM(page_table.shape, jnp.int32),
            pltpu.VMEM(queries.shape, BF16),
            pltpu.VMEM(key_scale.shape, F32),
            pltpu.VMEM((HEADS, keys // PAGE), jnp.int32),
            pltpu.VMEM((HEADS, keys), BF16),
            pltpu.VMEM(value_scale.shape, F32),
            pltpu.VMEM((pools, PAGE, LANES), BF16),
            pltpu.VMEM((pools, PAGE, LANES), BF16),
            pltpu.VMEM((keys, LANES), BF16),
            pltpu.VMEM((keys, LANES), BF16),
            pltpu.VMEM((3, HEADS, LANES), F32),
            pltpu.VMEM((keys // PAGE, HEADS, LANES), F32),
            pltpu.SemaphoreType.DMA((keys // BLOCK,)),
            pltpu.SemaphoreType.DMA((keys // BLOCK,)),
            pltpu.SemaphoreType.DMA((keys // BLOCK,)),
            pltpu.SemaphoreType.DMA((keys // BLOCK,)),
            pltpu.SemaphoreType.DMA((10,)),
        ],
        compiler_params=pltpu.CompilerParams(vmem_limit_bytes=PREPARE_LIMIT),
        cost_estimate=pl.CostEstimate(
            flops=2 * keys * LANES * LANES, bytes_accessed=10 * keys * LANES, transcendentals=0
        ),
        name="prepare",
    )(
        suffix_len,
        page_table,
        queries,
        key_scale,
        outlier_chan.reshape(-1, HEADS).T,
        outlier_val.reshape(-1, HEADS).T,
        value_scale,
        key_codes.reshape(keys, LANES),
        value_codes.reshape(keys, LANES),
        suffix_keys.reshape(pools, PAGE, LANES),
        suffix_values.reshape(pools, PAGE, LANES),
    )


def attend(place, all_queries, keys, values, own):
    rows = all_queries.shape[0]
    return pl.pallas_call(
        attend_kernel,
        out_shape=jax.ShapeDtypeStruct((rows // GROUP, GROUP + STATS, LANES), BF16),
        in_specs=[SMEM, VMEM, HBM, HBM, HBM],
        out_specs=VMEM,
        scratch_shapes=[
            pltpu.VMEM(own.shape[1:], F32),
            pltpu.VMEM(keys.shape, BF16),
            pltpu.VMEM(values.shape, BF16),
            pltpu.VMEM((keys.shape[0] // TILE, rows, TILE), F32),
            pltpu.VMEM((rows, LANES), F32),
            pltpu.VMEM((rows, LANES), F32),
            pltpu.VMEM((rows, LANES), F32),
            pltpu.SemaphoreType.DMA((keys.shape[0] // BLOCK,)),
            pltpu.SemaphoreType.DMA((2,)),
        ],
        compiler_params=pltpu.CompilerParams(vmem_limit_bytes=ATTEND_LIMIT),
        name="attend",
    )(place, all_queries, own, keys, values)


def shards(
    queries,
    key_codes,
    key_scale,
    outlier_chan,
    outlier_val,
    value_codes,
    value_scale,
    suffix_keys,
    suffix_values,
    page_table,
    suffix_len,
    out_weight,
):
    seq, near, far = ("zh", "zl", "y"), ("zl", "y"), "zh"
    samples = lax.axis_size(seq)
    queries = queries.reshape(HEADS, LANES)
    all_queries = spread(queries, seq).reshape(samples * HEADS, LANES)
    own = lax.axis_index(seq).astype(jnp.int32).reshape(1)
    params = pltpu.CompilerParams(vmem_limit_bytes=SMALL)
    prepared = prepare(
        queries,
        key_codes,
        key_scale,
        outlier_chan,
        outlier_val,
        value_codes,
        value_scale,
        suffix_keys,
        suffix_values,
        page_table,
        suffix_len,
    )
    partial = attend(own, all_queries, *prepared)
    partial = lax.all_to_all(partial, near, 0, 0)
    partial = pl.pallas_call(
        merge_kernel,
        out_shape=jax.ShapeDtypeStruct((lax.axis_size(far), GROUP + STATS, LANES), BF16),
        in_specs=[VMEM],
        out_specs=VMEM,
        compiler_params=params,
        name="merge_near",
    )(partial)
    partial = lax.all_to_all(partial, far, 0, 0)
    attention = pl.pallas_call(
        merge_kernel,
        out_shape=jax.ShapeDtypeStruct((lax.axis_size(near), GROUP, LANES), BF16),
        in_specs=[VMEM],
        out_specs=VMEM,
        compiler_params=params,
        name="merge_far",
    )(partial)
    attention = lax.all_to_all(attention, near, 0, 0)
    product = pl.pallas_call(
        project_kernel,
        out_shape=jax.ShapeDtypeStruct((samples, LANES), BF16),
        in_specs=[VMEM, VMEM],
        out_specs=VMEM,
        scratch_shapes=[pltpu.VMEM((samples * HEADS, LANES), F32)],
        compiler_params=params,
        name="project",
    )(attention, out_weight)
    tp = lax.axis_size("x") * lax.axis_size("core")
    product = lax.all_to_all(product.reshape(tp, samples // tp, LANES), ("x", "core"), 0, 0)
    return pl.pallas_call(
        sum_kernel,
        out_shape=jax.ShapeDtypeStruct((samples // tp, LANES), BF16),
        in_specs=[VMEM],
        out_specs=VMEM,
        compiler_params=params,
        name="sum_tp",
    )(product)


def solution(mesh):
    grid = Mesh(mesh.devices.reshape(8, 2, 4, 4, 2), ("zh", "zl", "y", "x", "core"))
    seq, tp = ("zh", "zl", "y"), ("x", "core")
    return jax.shard_map(
        shards,
        mesh=grid,
        in_specs=(
            P(seq, tp, None),
            P(seq, tp, None),
            P(seq, tp, None),
            P(seq, tp, None),
            P(seq, tp, None),
            P(seq, tp, None),
            P(seq, tp, None),
            P(seq, None, tp, None),
            P(seq, None, tp, None),
            P(seq, None),
            P(seq),
            P(tp, seq),
        ),
        out_specs=P(tp, seq),
        check_vma=False,
    )
```

```python
import functools
import math

import jax
import jax.numpy as jnp
from jax import lax
from jax.experimental import pallas as pl
from jax.experimental.pallas import tpu as pltpu
from jax.sharding import Mesh, PartitionSpec as P

F32 = jnp.float32
BF16 = jnp.bfloat16
LANES = 128
HEADS = 8
PAGE = 128
TILE = 256
BLOCK = 1024
ROOM = 256
PAGES = BLOCK // PAGE
SCORE_SCALE = math.log2(math.e) / math.sqrt(LANES)
SPLIT = 32
GROUP = 64
STATS = 16
LOW = -1e30
VMEM = pl.BlockSpec(memory_space=pltpu.VMEM)
SMEM = pl.BlockSpec(memory_space=pltpu.SMEM)
HBM = pl.BlockSpec(memory_space=pltpu.HBM)
PREPARE_LIMIT = 54 * 1024 * 1024
ATTEND_LIMIT = 53 * 1024 * 1024
SMALL = 4 * 1024 * 1024


def nt(a, b):
    return lax.dot_general(a, b, (((1,), (1,)), ((), ())), preferred_element_type=F32)


def split_rows(row):
    high = row.astype(BF16).astype(F32)
    rest = row - high
    middle = rest.astype(BF16).astype(F32)
    low = rest - middle
    part = lax.broadcasted_iota(jnp.int32, row.shape, row.ndim - 1) // SPLIT
    kept = jnp.where(part == 0, high, jnp.where(part == 1, middle, low))
    return jnp.where(part < 3, kept, 0.0).astype(BF16)


def to_lanes(columns):
    row = lax.broadcasted_iota(jnp.int32, columns.shape, 0)
    lane = lax.broadcasted_iota(jnp.int32, columns.shape, 1)
    return jnp.sum(jnp.where(lane % SPLIT == row, columns, 0.0), axis=0, keepdims=True)


def stat_rows(logs):
    copies = STATS * SPLIT // GROUP
    rows = [
        jnp.broadcast_to(to_lanes(logs[at : at + SPLIT]), (copies, LANES))
        for at in range(0, GROUP, SPLIT)
    ]
    return split_rows(jnp.concatenate(rows, axis=0))


def to_rows(stat):
    wide = jnp.broadcast_to(stat, (SPLIT, LANES))
    row = lax.broadcasted_iota(jnp.int32, wide.shape, 0)
    lane = lax.broadcasted_iota(jnp.int32, wide.shape, 1)
    return jnp.sum(jnp.where(lane % SPLIT == row, wide, 0.0), axis=1, keepdims=True)


def prepare_kernel(
    len_hbm,
    table_hbm,
    own_q_hbm,
    kscale_hbm,
    chan_hbm,
    outlier_hbm,
    vscale_hbm,
    kcodes_hbm,
    vcodes_hbm,
    skeys_hbm,
    svalues_hbm,
    keys_hbm,
    values_hbm,
    own_hbm,
    len_ref,
    table_ref,
    own_q_ref,
    kscale_ref,
    chan_ref,
    outlier_ref,
    vscale_ref,
    skbuf,
    svbuf,
    kbuf,
    vbuf,
    own_ref,
    onehot,
    ksem,
    vsem,
    kout,
    vout,
    sem,
):
    blocks = kbuf.shape[0] // BLOCK

    def block_rows(i):
        return pl.ds(pl.multiple_of(i * BLOCK, BLOCK), BLOCK)

    def chunk(hbm, buf, sems, i):
        return pltpu.make_async_copy(hbm.at[block_rows(i), :], buf.at[block_rows(i), :], sems.at[i])

    small = [
        pltpu.make_async_copy(source, target, sem.at[n])
        for n, (source, target) in enumerate(
            (
                (chan_hbm, chan_ref),
                (outlier_hbm, outlier_ref),
                (kscale_hbm, kscale_ref),
                (vscale_hbm, vscale_ref),
                (own_q_hbm, own_q_ref),
                (skeys_hbm, skbuf),
                (svalues_hbm, svbuf),
                (len_hbm, len_ref),
                (table_hbm, table_ref),
            )
        )
    ]
    result = pltpu.make_async_copy(own_ref, own_hbm.at[0], sem.at[len(small)])
    for copy in small[:3]:
        copy.start()
    for i in range(blocks):
        chunk(kcodes_hbm, kbuf, ksem, i).start()
    for copy in small[3:]:
        copy.start()
    for i in range(blocks):
        chunk(vcodes_hbm, vbuf, vsem, i).start()
    small[0].wait()

    lane = lax.broadcasted_iota(jnp.int32, (HEADS, LANES), 1)
    channels = chan_ref[...]
    for page in range(onehot.shape[0]):
        onehot[page] = (lane == channels[:, page : page + 1]).astype(F32)
    none = jnp.zeros((HEADS, LANES), F32)
    for copy in small[1:3]:
        copy.wait()

    @pl.loop(0, blocks)
    def key_block(i):
        chunk(kcodes_hbm, kbuf, ksem, i).wait()
        first_page = i * PAGES
        slots = [
            outlier_ref[:, pl.ds(pl.multiple_of((first_page + p) * PAGE, PAGE), PAGE)].astype(F32)
            for p in range(PAGES)
        ]
        slots = jnp.concatenate(slots + [none] * (LANES // HEADS - PAGES), axis=0).T.astype(BF16)
        chosen = []
        for p in range(PAGES):
            column = [none] * (LANES // HEADS)
            column[p] = onehot[first_page + p]
            chosen.append(jnp.concatenate(column, axis=0).astype(BF16))
        correction = jnp.dot(slots, jnp.concatenate(chosen, axis=1), preferred_element_type=F32)
        for p in range(PAGES):
            rows = pl.ds(pl.multiple_of((first_page + p) * PAGE, PAGE), PAGE)
            base = kbuf[rows, :].astype(F32) * kscale_ref[first_page + p]
            kbuf[rows, :] = (base + correction[:, p * LANES : (p + 1) * LANES]).astype(BF16)
        pltpu.make_async_copy(
            kbuf.at[block_rows(i), :], keys_hbm.at[block_rows(i), :], kout.at[i]
        ).start()

    for copy in small[3:]:
        copy.wait()
    live = len_ref[0]
    own_scores = [
        jnp.where(
            lane + j * PAGE < live,
            nt(own_q_ref[...], skbuf[table_ref[0, j]]) * SCORE_SCALE,
            LOW,
        )
        for j in range(skbuf.shape[0])
    ]
    top = functools.reduce(jnp.maximum, own_scores)
    top = jnp.max(top, axis=1, keepdims=True)
    sums = jnp.zeros((HEADS, LANES), F32)
    weighted = jnp.zeros((HEADS, LANES), F32)
    for j, part in enumerate(own_scores):
        weight = jnp.where(lane + j * PAGE < live, jnp.exp2(part - top), 0.0)
        sums = sums + weight
        weighted = weighted + jnp.dot(
            weight.astype(BF16), svbuf[table_ref[0, j]], preferred_element_type=F32
        )
    own_ref[0] = jnp.broadcast_to(top, (HEADS, LANES))
    own_ref[1] = jnp.broadcast_to(jnp.sum(sums, axis=1, keepdims=True), (HEADS, LANES))
    own_ref[2] = weighted
    result.start()

    @pl.loop(0, blocks)
    def value_block(i):
        chunk(vcodes_hbm, vbuf, vsem, i).wait()
        for p in range(PAGES):
            rows = pl.ds(pl.multiple_of((i * PAGES + p) * PAGE, PAGE), PAGE)
            vbuf[rows, :] = (vbuf[rows, :].astype(F32) * vscale_ref[i * PAGES + p]).astype(BF16)
        pltpu.make_async_copy(
            vbuf.at[block_rows(i), :], values_hbm.at[block_rows(i), :], vout.at[i]
        ).start()

    for i in range(blocks):
        pltpu.make_async_copy(
            kbuf.at[block_rows(i), :], keys_hbm.at[block_rows(i), :], kout.at[i]
        ).wait()
        pltpu.make_async_copy(
            vbuf.at[block_rows(i), :], values_hbm.at[block_rows(i), :], vout.at[i]
        ).wait()
    result.wait()


def attend_kernel(
    place_ref,
    q_ref,
    own_hbm,
    keys_hbm,
    values_hbm,
    out_ref,
    own_ref,
    keys_ref,
    values_ref,
    scores,
    peak,
    total,
    acc,
    ksem,
    sem,
):
    load = pltpu.make_async_copy(values_hbm, values_ref, sem.at[0])
    own_load = pltpu.make_async_copy(own_hbm.at[0], own_ref, sem.at[1])

    def chunk(i):
        rows = pl.ds(pl.multiple_of(i * BLOCK, BLOCK), BLOCK)
        return pltpu.make_async_copy(keys_hbm.at[rows, :], keys_ref.at[rows, :], ksem.at[i])

    for i in range(keys_ref.shape[0] // BLOCK):
        chunk(i).start()
    load.start()
    own_load.start()
    blocks = keys_ref.shape[0] // BLOCK
    queries = q_ref.shape[0]
    peak[...] = jnp.full(peak.shape, LOW, F32)

    @pl.loop(0, blocks)
    def score_block(i):
        chunk(i).wait()
        running = peak[...]
        for j in range(BLOCK // TILE):
            rows = pl.ds(pl.multiple_of(i * BLOCK + j * TILE, TILE), TILE)
            tile = nt(q_ref[...], keys_ref[rows, :])
            scores[i * (BLOCK // TILE) + j] = tile
            running = jnp.maximum(running, jnp.maximum(tile[:, :LANES], tile[:, LANES:]))
        peak[...] = running

    peak[...] = jnp.broadcast_to(
        jnp.max(peak[...], axis=1, keepdims=True) * SCORE_SCALE, peak.shape
    )
    total[...] = jnp.zeros(total.shape, F32)
    acc[...] = jnp.zeros(acc.shape, F32)
    load.wait()
    own_load.wait()

    @pl.loop(0, blocks, unroll=True)
    def value_block(i):
        running = total[...]
        top = peak[...]
        weights = []
        for j in range(BLOCK // TILE):
            for p in range(TILE // PAGE):
                part = scores[i * (BLOCK // TILE) + j, :, p * LANES : (p + 1) * LANES]
                weight = jnp.exp2(part * SCORE_SCALE - top)
                running = running + weight
                weights.append(weight.astype(BF16))
        total[...] = running
        rows = pl.ds(pl.multiple_of(i * BLOCK, BLOCK), BLOCK)
        acc[...] += jnp.dot(
            jnp.concatenate(weights, axis=1), values_ref[rows, :], preferred_element_type=F32
        )

    total[...] = jnp.broadcast_to(jnp.sum(total[...], axis=1, keepdims=True), total.shape)

    own = pl.ds(pl.multiple_of(place_ref[0] * HEADS, HEADS), HEADS)
    top = jnp.maximum(peak[own, :], own_ref[0])
    fade, own_fade = jnp.exp2(peak[own, :] - top), jnp.exp2(own_ref[0] - top)
    peak[own, :] = top
    total[own, :] = total[own, :] * fade + own_ref[1] * own_fade
    acc[own, :] = acc[own, :] * fade + own_ref[2] * own_fade

    pieces = out_ref.shape[0]
    for c in range(pieces):
        rows = [
            slice((u * pieces + c) * HEADS, (u * pieces + c + 1) * HEADS)
            for u in range(GROUP // HEADS)
        ]
        part = [acc[r, :] / total[r, :] for r in rows]
        logs = [peak[r, :] + jnp.log2(total[r, :]) for r in rows]
        out_ref[c, :GROUP, :] = jnp.concatenate(part, axis=0).astype(BF16)
        out_ref[c, GROUP:, :] = stat_rows(jnp.concatenate(logs, axis=0))


def merge_kernel(in_ref, out_ref):
    sources = in_ref.shape[0]
    logs = []
    for s in range(sources):
        stats = in_ref[s, GROUP:, :].astype(F32)
        first = [at * STATS // GROUP for at in range(0, GROUP, SPLIT)]
        logs.append(jnp.concatenate([to_rows(stats[at : at + 1]) for at in first], axis=0))
    top = functools.reduce(jnp.maximum, logs)
    sums = jnp.zeros(top.shape, F32)
    weighted = jnp.zeros((GROUP, LANES), F32)
    for s in range(sources):
        weight = jnp.exp2(logs[s] - top)
        sums = sums + weight
        weighted = weighted + in_ref[s, :GROUP, :].astype(F32) * weight
    merged = (weighted / sums).astype(BF16)
    copies, rows, lanes = out_ref.shape
    if rows > GROUP:
        stat = stat_rows(jnp.broadcast_to(top + jnp.log2(sums), (GROUP, LANES)))
    for c in range(copies):
        out_ref[c, :GROUP, :] = merged
        if rows > GROUP:
            out_ref[c, GROUP:, :] = stat


def project_kernel(in_ref, weight_ref, out_ref, wide):
    blocks = in_ref.shape[0]
    for c in range(blocks):
        block = in_ref[c].astype(F32)
        for u in range(GROUP // HEADS):
            first = (u * blocks + c) * HEADS
            wide[first : first + HEADS, :] = block[u * HEADS : (u + 1) * HEADS]
    samples = blocks * GROUP // HEADS
    result = jnp.zeros((samples, LANES), F32)
    for h in range(HEADS):
        part = wide[pl.ds(h, samples, stride=HEADS), :].astype(BF16)
        result = result + jnp.dot(
            part, weight_ref[h * LANES : (h + 1) * LANES, :], preferred_element_type=F32
        )
    out_ref[...] = result.astype(BF16)


def sum_kernel(in_ref, out_ref):
    result = in_ref[0].astype(F32)
    for c in range(1, in_ref.shape[0]):
        result = result + in_ref[c].astype(F32)
    out_ref[...] = result.astype(BF16)


def spread(block, axis):
    copies = jnp.broadcast_to(block[None], (lax.axis_size(axis),) + block.shape)
    return lax.all_to_all(copies, axis, 0, 0)


def prepare(
    queries,
    key_codes,
    key_scale,
    outlier_chan,
    outlier_val,
    value_codes,
    value_scale,
    suffix_keys,
    suffix_values,
    page_table,
    suffix_len,
):
    keys = key_codes.shape[0]
    pools = suffix_keys.shape[0]
    return pl.pallas_call(
        prepare_kernel,
        out_shape=(
            jax.ShapeDtypeStruct((keys, LANES), BF16),
            jax.ShapeDtypeStruct((keys, LANES), BF16),
            jax.ShapeDtypeStruct((ROOM, 3, HEADS, LANES), F32),
        ),
        in_specs=[HBM] * 11,
        out_specs=(HBM, HBM, HBM),
        scratch_shapes=[
            pltpu.SMEM(suffix_len.shape, jnp.int32),
            pltpu.SMEM(page_table.shape, jnp.int32),
            pltpu.VMEM(queries.shape, BF16),
            pltpu.VMEM(key_scale.shape, F32),
            pltpu.VMEM((HEADS, keys // PAGE), jnp.int32),
            pltpu.VMEM((HEADS, keys), BF16),
            pltpu.VMEM(value_scale.shape, F32),
            pltpu.VMEM((pools, PAGE, LANES), BF16),
            pltpu.VMEM((pools, PAGE, LANES), BF16),
            pltpu.VMEM((keys, LANES), BF16),
            pltpu.VMEM((keys, LANES), BF16),
            pltpu.VMEM((3, HEADS, LANES), F32),
            pltpu.VMEM((keys // PAGE, HEADS, LANES), F32),
            pltpu.SemaphoreType.DMA((keys // BLOCK,)),
            pltpu.SemaphoreType.DMA((keys // BLOCK,)),
            pltpu.SemaphoreType.DMA((keys // BLOCK,)),
            pltpu.SemaphoreType.DMA((keys // BLOCK,)),
            pltpu.SemaphoreType.DMA((10,)),
        ],
        compiler_params=pltpu.CompilerParams(vmem_limit_bytes=PREPARE_LIMIT),
        cost_estimate=pl.CostEstimate(
            flops=2 * keys * LANES * LANES, bytes_accessed=10 * keys * LANES, transcendentals=0
        ),
        name="prepare",
    )(
        suffix_len,
        page_table,
        queries,
        key_scale,
        outlier_chan.reshape(-1, HEADS).T,
        outlier_val.reshape(-1, HEADS).T,
        value_scale,
        key_codes.reshape(keys, LANES),
        value_codes.reshape(keys, LANES),
        suffix_keys.reshape(pools, PAGE, LANES),
        suffix_values.reshape(pools, PAGE, LANES),
    )


def attend(place, all_queries, keys, values, own):
    rows = all_queries.shape[0]
    return pl.pallas_call(
        attend_kernel,
        out_shape=jax.ShapeDtypeStruct((rows // GROUP, GROUP + STATS, LANES), BF16),
        in_specs=[SMEM, VMEM, HBM, HBM, HBM],
        out_specs=VMEM,
        scratch_shapes=[
            pltpu.VMEM(own.shape[1:], F32),
            pltpu.VMEM(keys.shape, BF16),
            pltpu.VMEM(values.shape, BF16),
            pltpu.VMEM((keys.shape[0] // TILE, rows, TILE), F32),
            pltpu.VMEM((rows, LANES), F32),
            pltpu.VMEM((rows, LANES), F32),
            pltpu.VMEM((rows, LANES), F32),
            pltpu.SemaphoreType.DMA((keys.shape[0] // BLOCK,)),
            pltpu.SemaphoreType.DMA((2,)),
        ],
        compiler_params=pltpu.CompilerParams(vmem_limit_bytes=ATTEND_LIMIT),
        name="attend",
    )(place, all_queries, own, keys, values)


def shards(
    queries,
    key_codes,
    key_scale,
    outlier_chan,
    outlier_val,
    value_codes,
    value_scale,
    suffix_keys,
    suffix_values,
    page_table,
    suffix_len,
    out_weight,
):
    seq, near, far = ("zh", "zl", "y"), ("zl", "y"), "zh"
    samples = lax.axis_size(seq)
    queries = queries.reshape(HEADS, LANES)
    all_queries = spread(spread(queries, near), far).reshape(samples * HEADS, LANES)
    own = lax.axis_index(seq).astype(jnp.int32).reshape(1)
    params = pltpu.CompilerParams(vmem_limit_bytes=SMALL)
    prepared = prepare(
        queries,
        key_codes,
        key_scale,
        outlier_chan,
        outlier_val,
        value_codes,
        value_scale,
        suffix_keys,
        suffix_values,
        page_table,
        suffix_len,
    )
    partial = attend(own, all_queries, *prepared)
    partial = lax.all_to_all(partial, near, 0, 0)
    partial = pl.pallas_call(
        merge_kernel,
        out_shape=jax.ShapeDtypeStruct((lax.axis_size(far), GROUP + STATS, LANES), BF16),
        in_specs=[VMEM],
        out_specs=VMEM,
        compiler_params=params,
        name="merge_near",
    )(partial)
    partial = lax.all_to_all(partial, far, 0, 0)
    attention = pl.pallas_call(
        merge_kernel,
        out_shape=jax.ShapeDtypeStruct((lax.axis_size(near), GROUP, LANES), BF16),
        in_specs=[VMEM],
        out_specs=VMEM,
        compiler_params=params,
        name="merge_far",
    )(partial)
    attention = lax.all_to_all(attention, near, 0, 0)
    product = pl.pallas_call(
        project_kernel,
        out_shape=jax.ShapeDtypeStruct((samples, LANES), BF16),
        in_specs=[VMEM, VMEM],
        out_specs=VMEM,
        scratch_shapes=[pltpu.VMEM((samples * HEADS, LANES), F32)],
        compiler_params=params,
        name="project",
    )(attention, out_weight)
    tp = lax.axis_size("x") * lax.axis_size("core")
    product = lax.all_to_all(product.reshape(tp, samples // tp, LANES), ("x", "core"), 0, 0)
    return pl.pallas_call(
        sum_kernel,
        out_shape=jax.ShapeDtypeStruct((samples // tp, LANES), BF16),
        in_specs=[VMEM],
        out_specs=VMEM,
        compiler_params=params,
        name="sum_tp",
    )(product)


def solution(mesh):
    grid = Mesh(mesh.devices.reshape(8, 2, 4, 4, 2), ("zh", "zl", "y", "x", "core"))
    seq, tp = ("zh", "zl", "y"), ("x", "core")
    return jax.shard_map(
        shards,
        mesh=grid,
        in_specs=(
            P(seq, tp, None),
            P(seq, tp, None),
            P(seq, tp, None),
            P(seq, tp, None),
            P(seq, tp, None),
            P(seq, tp, None),
            P(seq, tp, None),
            P(seq, None, tp, None),
            P(seq, None, tp, None),
            P(seq, None),
            P(seq),
            P(tp, seq),
        ),
        out_specs=P(tp, seq),
        check_vma=False,
    )
```

```python
import functools
import math

import jax
import jax.numpy as jnp
from jax import lax
from jax.experimental import pallas as pl
from jax.experimental.pallas import tpu as pltpu
from jax.sharding import Mesh, PartitionSpec as P

F32 = jnp.float32
BF16 = jnp.bfloat16
LANES = 128
HEADS = 8
PAGE = 128
TILE = 256
BLOCK = 2048
WEIGHT_STEP = 1024
ROOM = 256
PAGES = BLOCK // PAGE
SCORE_SCALE = math.log2(math.e) / math.sqrt(LANES)
SPLIT = 32
GROUP = 64
STATS = 8
LOW = -1e30
VMEM = pl.BlockSpec(memory_space=pltpu.VMEM)
SMEM = pl.BlockSpec(memory_space=pltpu.SMEM)
HBM = pl.BlockSpec(memory_space=pltpu.HBM)
PREPARE_LIMIT = 54 * 1024 * 1024
ATTEND_LIMIT = 53 * 1024 * 1024
SMALL = 4 * 1024 * 1024


def nt(a, b):
    return lax.dot_general(a, b, (((1,), (1,)), ((), ())), preferred_element_type=F32)


def split_rows(row):
    high = row.astype(BF16).astype(F32)
    rest = row - high
    middle = rest.astype(BF16).astype(F32)
    low = rest - middle
    part = lax.broadcasted_iota(jnp.int32, row.shape, row.ndim - 1) // SPLIT
    kept = jnp.where(part == 0, high, jnp.where(part == 1, middle, low))
    return jnp.where(part < 3, kept, 0.0).astype(BF16)


def to_lanes(columns):
    row = lax.broadcasted_iota(jnp.int32, columns.shape, 0)
    lane = lax.broadcasted_iota(jnp.int32, columns.shape, 1)
    return jnp.sum(jnp.where(lane % SPLIT == row, columns, 0.0), axis=0, keepdims=True)


def stat_rows(logs):
    copies = STATS * SPLIT // GROUP
    rows = [
        jnp.broadcast_to(to_lanes(logs[at : at + SPLIT]), (copies, LANES))
        for at in range(0, GROUP, SPLIT)
    ]
    return split_rows(jnp.concatenate(rows, axis=0))


def to_rows(stat):
    wide = jnp.broadcast_to(stat, (SPLIT, LANES))
    row = lax.broadcasted_iota(jnp.int32, wide.shape, 0)
    lane = lax.broadcasted_iota(jnp.int32, wide.shape, 1)
    return jnp.sum(jnp.where(lane % SPLIT == row, wide, 0.0), axis=1, keepdims=True)


def prepare_kernel(
    len_hbm,
    table_hbm,
    own_q_hbm,
    kscale_hbm,
    chan_hbm,
    outlier_hbm,
    vscale_hbm,
    kcodes_hbm,
    vcodes_hbm,
    skeys_hbm,
    svalues_hbm,
    keys_hbm,
    values_hbm,
    own_hbm,
    len_ref,
    table_ref,
    own_q_ref,
    kscale_ref,
    chan_ref,
    outlier_ref,
    vscale_ref,
    skbuf,
    svbuf,
    kbuf,
    vbuf,
    own_ref,
    onehot,
    ksem,
    vsem,
    kout,
    vout,
    sem,
):
    blocks = kbuf.shape[0] // BLOCK

    def block_rows(i):
        return pl.ds(pl.multiple_of(i * BLOCK, BLOCK), BLOCK)

    def chunk(hbm, buf, sems, i):
        return pltpu.make_async_copy(hbm.at[block_rows(i), :], buf.at[block_rows(i), :], sems.at[i])

    small = [
        pltpu.make_async_copy(source, target, sem.at[n])
        for n, (source, target) in enumerate(
            (
                (chan_hbm, chan_ref),
                (outlier_hbm, outlier_ref),
                (kscale_hbm, kscale_ref),
                (vscale_hbm, vscale_ref),
                (own_q_hbm, own_q_ref),
                (skeys_hbm, skbuf),
                (svalues_hbm, svbuf),
                (len_hbm, len_ref),
                (table_hbm, table_ref),
            )
        )
    ]
    result = pltpu.make_async_copy(own_ref, own_hbm.at[0], sem.at[len(small)])
    for copy in small[:3]:
        copy.start()
    for i in range(blocks):
        chunk(kcodes_hbm, kbuf, ksem, i).start()
    for copy in small[3:]:
        copy.start()
    for i in range(blocks):
        chunk(vcodes_hbm, vbuf, vsem, i).start()
    small[0].wait()

    lane = lax.broadcasted_iota(jnp.int32, (HEADS, LANES), 1)
    channels = chan_ref[...]
    for page in range(onehot.shape[0]):
        onehot[page] = (lane == channels[:, page : page + 1]).astype(F32)
    none = jnp.zeros((HEADS, LANES), F32)
    for copy in small[1:3]:
        copy.wait()

    @pl.loop(0, blocks)
    def key_block(i):
        chunk(kcodes_hbm, kbuf, ksem, i).wait()
        first_page = i * PAGES
        slots = [
            outlier_ref[:, pl.ds(pl.multiple_of((first_page + p) * PAGE, PAGE), PAGE)].astype(F32)
            for p in range(PAGES)
        ]
        slots = jnp.concatenate(slots + [none] * (LANES // HEADS - PAGES), axis=0).T.astype(BF16)
        chosen = []
        for p in range(PAGES):
            column = [none] * (LANES // HEADS)
            column[p] = onehot[first_page + p]
            chosen.append(jnp.concatenate(column, axis=0).astype(BF16))
        correction = jnp.dot(slots, jnp.concatenate(chosen, axis=1), preferred_element_type=F32)
        for p in range(PAGES):
            rows = pl.ds(pl.multiple_of((first_page + p) * PAGE, PAGE), PAGE)
            base = kbuf[rows, :].astype(F32) * kscale_ref[first_page + p]
            kbuf[rows, :] = (base + correction[:, p * LANES : (p + 1) * LANES]).astype(BF16)
        pltpu.make_async_copy(
            kbuf.at[block_rows(i), :], keys_hbm.at[block_rows(i), :], kout.at[i]
        ).start()

    for copy in small[3:]:
        copy.wait()
    live = len_ref[0]
    own_scores = [
        jnp.where(
            lane + j * PAGE < live,
            nt(own_q_ref[...], skbuf[table_ref[0, j]]) * SCORE_SCALE,
            LOW,
        )
        for j in range(skbuf.shape[0])
    ]
    top = functools.reduce(jnp.maximum, own_scores)
    top = jnp.max(top, axis=1, keepdims=True)
    sums = jnp.zeros((HEADS, LANES), F32)
    weighted = jnp.zeros((HEADS, LANES), F32)
    for j, part in enumerate(own_scores):
        weight = jnp.where(lane + j * PAGE < live, jnp.exp2(part - top), 0.0)
        sums = sums + weight
        weighted = weighted + jnp.dot(
            weight.astype(BF16), svbuf[table_ref[0, j]], preferred_element_type=F32
        )
    own_ref[0] = jnp.broadcast_to(top, (HEADS, LANES))
    own_ref[1] = jnp.broadcast_to(jnp.sum(sums, axis=1, keepdims=True), (HEADS, LANES))
    own_ref[2] = weighted
    result.start()

    @pl.loop(0, blocks)
    def value_block(i):
        chunk(vcodes_hbm, vbuf, vsem, i).wait()
        for p in range(PAGES):
            rows = pl.ds(pl.multiple_of((i * PAGES + p) * PAGE, PAGE), PAGE)
            vbuf[rows, :] = (vbuf[rows, :].astype(F32) * vscale_ref[i * PAGES + p]).astype(BF16)
        pltpu.make_async_copy(
            vbuf.at[block_rows(i), :], values_hbm.at[block_rows(i), :], vout.at[i]
        ).start()

    for i in range(blocks):
        pltpu.make_async_copy(
            kbuf.at[block_rows(i), :], keys_hbm.at[block_rows(i), :], kout.at[i]
        ).wait()
        pltpu.make_async_copy(
            vbuf.at[block_rows(i), :], values_hbm.at[block_rows(i), :], vout.at[i]
        ).wait()
    result.wait()


def attend_kernel(
    place_ref,
    q_ref,
    own_hbm,
    keys_hbm,
    values_hbm,
    out_ref,
    own_ref,
    keys_ref,
    values_ref,
    scores,
    peak,
    total,
    acc,
    ksem,
    sem,
):
    load = pltpu.make_async_copy(values_hbm, values_ref, sem.at[0])
    own_load = pltpu.make_async_copy(own_hbm.at[0], own_ref, sem.at[1])

    def chunk(i):
        rows = pl.ds(pl.multiple_of(i * BLOCK, BLOCK), BLOCK)
        return pltpu.make_async_copy(keys_hbm.at[rows, :], keys_ref.at[rows, :], ksem.at[i])

    for i in range(keys_ref.shape[0] // BLOCK):
        chunk(i).start()
    load.start()
    own_load.start()
    blocks = keys_ref.shape[0] // BLOCK
    queries = q_ref.shape[0]
    peak[...] = jnp.full(peak.shape, LOW, F32)

    @pl.loop(0, blocks)
    def score_block(i):
        chunk(i).wait()
        running = peak[...]
        for j in range(BLOCK // TILE):
            rows = pl.ds(pl.multiple_of(i * BLOCK + j * TILE, TILE), TILE)
            tile = nt(q_ref[...], keys_ref[rows, :])
            scores[i * (BLOCK // TILE) + j] = tile
            running = jnp.maximum(running, jnp.maximum(tile[:, :LANES], tile[:, LANES:]))
        peak[...] = running

    peak[...] = jnp.broadcast_to(
        jnp.max(peak[...], axis=1, keepdims=True) * SCORE_SCALE, peak.shape
    )
    total[...] = jnp.zeros(total.shape, F32)
    acc[...] = jnp.zeros(acc.shape, F32)
    load.wait()
    own_load.wait()

    @pl.loop(0, keys_ref.shape[0] // WEIGHT_STEP, unroll=True)
    def value_block(i):
        running = total[...]
        top = peak[...]
        weights = []
        for j in range(WEIGHT_STEP // TILE):
            for p in range(TILE // PAGE):
                part = scores[i * (WEIGHT_STEP // TILE) + j, :, p * LANES : (p + 1) * LANES]
                weight = jnp.exp2(part * SCORE_SCALE - top)
                running = running + weight
                weights.append(weight.astype(BF16))
        total[...] = running
        rows = pl.ds(pl.multiple_of(i * WEIGHT_STEP, WEIGHT_STEP), WEIGHT_STEP)
        acc[...] += jnp.dot(
            jnp.concatenate(weights, axis=1), values_ref[rows, :], preferred_element_type=F32
        )

    total[...] = jnp.broadcast_to(jnp.sum(total[...], axis=1, keepdims=True), total.shape)

    own = pl.ds(pl.multiple_of(place_ref[0] * HEADS, HEADS), HEADS)
    top = jnp.maximum(peak[own, :], own_ref[0])
    fade, own_fade = jnp.exp2(peak[own, :] - top), jnp.exp2(own_ref[0] - top)
    peak[own, :] = top
    total[own, :] = total[own, :] * fade + own_ref[1] * own_fade
    acc[own, :] = acc[own, :] * fade + own_ref[2] * own_fade

    pieces = out_ref.shape[0]
    for c in range(pieces):
        rows = [
            slice((u * pieces + c) * HEADS, (u * pieces + c + 1) * HEADS)
            for u in range(GROUP // HEADS)
        ]
        part = [acc[r, :] / total[r, :] for r in rows]
        logs = [peak[r, :] + jnp.log2(total[r, :]) for r in rows]
        out_ref[c, :GROUP, :] = jnp.concatenate(part, axis=0).astype(BF16)
        out_ref[c, GROUP:, :] = stat_rows(jnp.concatenate(logs, axis=0))


def merge_kernel(in_ref, out_ref):
    sources = in_ref.shape[0]
    logs = []
    for s in range(sources):
        stats = in_ref[s, GROUP:, :].astype(F32)
        first = [at * STATS // GROUP for at in range(0, GROUP, SPLIT)]
        logs.append(jnp.concatenate([to_rows(stats[at : at + 1]) for at in first], axis=0))
    top = functools.reduce(jnp.maximum, logs)
    sums = jnp.zeros(top.shape, F32)
    weighted = jnp.zeros((GROUP, LANES), F32)
    for s in range(sources):
        weight = jnp.exp2(logs[s] - top)
        sums = sums + weight
        weighted = weighted + in_ref[s, :GROUP, :].astype(F32) * weight
    merged = (weighted / sums).astype(BF16)
    copies, rows, lanes = out_ref.shape
    if rows > GROUP:
        stat = stat_rows(jnp.broadcast_to(top + jnp.log2(sums), (GROUP, LANES)))
    for c in range(copies):
        out_ref[c, :GROUP, :] = merged
        if rows > GROUP:
            out_ref[c, GROUP:, :] = stat


def project_kernel(in_ref, weight_ref, out_ref, wide):
    blocks = in_ref.shape[0]
    for c in range(blocks):
        block = in_ref[c].astype(F32)
        for u in range(GROUP // HEADS):
            first = (u * blocks + c) * HEADS
            wide[first : first + HEADS, :] = block[u * HEADS : (u + 1) * HEADS]
    samples = blocks * GROUP // HEADS
    result = jnp.zeros((samples, LANES), F32)
    for h in range(HEADS):
        part = wide[pl.ds(h, samples, stride=HEADS), :].astype(BF16)
        result = result + jnp.dot(
            part, weight_ref[h * LANES : (h + 1) * LANES, :], preferred_element_type=F32
        )
    out_ref[...] = result.astype(BF16)


def sum_kernel(in_ref, out_ref):
    result = in_ref[0].astype(F32)
    for c in range(1, in_ref.shape[0]):
        result = result + in_ref[c].astype(F32)
    out_ref[...] = result.astype(BF16)


def spread(block, axis):
    copies = jnp.broadcast_to(block[None], (lax.axis_size(axis),) + block.shape)
    return lax.all_to_all(copies, axis, 0, 0)


def prepare(
    queries,
    key_codes,
    key_scale,
    outlier_chan,
    outlier_val,
    value_codes,
    value_scale,
    suffix_keys,
    suffix_values,
    page_table,
    suffix_len,
):
    keys = key_codes.shape[0]
    pools = suffix_keys.shape[0]
    return pl.pallas_call(
        prepare_kernel,
        out_shape=(
            jax.ShapeDtypeStruct((keys, LANES), BF16),
            jax.ShapeDtypeStruct((keys, LANES), BF16),
            jax.ShapeDtypeStruct((ROOM, 3, HEADS, LANES), F32),
        ),
        in_specs=[HBM] * 11,
        out_specs=(HBM, HBM, HBM),
        scratch_shapes=[
            pltpu.SMEM(suffix_len.shape, jnp.int32),
            pltpu.SMEM(page_table.shape, jnp.int32),
            pltpu.VMEM(queries.shape, BF16),
            pltpu.VMEM(key_scale.shape, F32),
            pltpu.VMEM((HEADS, keys // PAGE), jnp.int32),
            pltpu.VMEM((HEADS, keys), BF16),
            pltpu.VMEM(value_scale.shape, F32),
            pltpu.VMEM((pools, PAGE, LANES), BF16),
            pltpu.VMEM((pools, PAGE, LANES), BF16),
            pltpu.VMEM((keys, LANES), BF16),
            pltpu.VMEM((keys, LANES), BF16),
            pltpu.VMEM((3, HEADS, LANES), F32),
            pltpu.VMEM((keys // PAGE, HEADS, LANES), F32),
            pltpu.SemaphoreType.DMA((keys // BLOCK,)),
            pltpu.SemaphoreType.DMA((keys // BLOCK,)),
            pltpu.SemaphoreType.DMA((keys // BLOCK,)),
            pltpu.SemaphoreType.DMA((keys // BLOCK,)),
            pltpu.SemaphoreType.DMA((10,)),
        ],
        compiler_params=pltpu.CompilerParams(vmem_limit_bytes=PREPARE_LIMIT),
        cost_estimate=pl.CostEstimate(
            flops=2 * keys * LANES * LANES, bytes_accessed=10 * keys * LANES, transcendentals=0
        ),
        name="prepare",
    )(
        suffix_len,
        page_table,
        queries,
        key_scale,
        outlier_chan.reshape(-1, HEADS).T,
        outlier_val.reshape(-1, HEADS).T,
        value_scale,
        key_codes.reshape(keys, LANES),
        value_codes.reshape(keys, LANES),
        suffix_keys.reshape(pools, PAGE, LANES),
        suffix_values.reshape(pools, PAGE, LANES),
    )


def attend(place, all_queries, keys, values, own):
    rows = all_queries.shape[0]
    return pl.pallas_call(
        attend_kernel,
        out_shape=jax.ShapeDtypeStruct((rows // GROUP, GROUP + STATS, LANES), BF16),
        in_specs=[SMEM, VMEM, HBM, HBM, HBM],
        out_specs=VMEM,
        scratch_shapes=[
            pltpu.VMEM(own.shape[1:], F32),
            pltpu.VMEM(keys.shape, BF16),
            pltpu.VMEM(values.shape, BF16),
            pltpu.VMEM((keys.shape[0] // TILE, rows, TILE), F32),
            pltpu.VMEM((rows, LANES), F32),
            pltpu.VMEM((rows, LANES), F32),
            pltpu.VMEM((rows, LANES), F32),
            pltpu.SemaphoreType.DMA((keys.shape[0] // BLOCK,)),
            pltpu.SemaphoreType.DMA((2,)),
        ],
        compiler_params=pltpu.CompilerParams(vmem_limit_bytes=ATTEND_LIMIT),
        name="attend",
    )(place, all_queries, own, keys, values)


def shards(
    queries,
    key_codes,
    key_scale,
    outlier_chan,
    outlier_val,
    value_codes,
    value_scale,
    suffix_keys,
    suffix_values,
    page_table,
    suffix_len,
    out_weight,
):
    seq, near, far = ("zh", "zl", "y"), ("zl", "y"), "zh"
    samples = lax.axis_size(seq)
    queries = queries.reshape(HEADS, LANES)
    all_queries = spread(queries, seq).reshape(samples * HEADS, LANES)
    own = lax.axis_index(seq).astype(jnp.int32).reshape(1)
    params = pltpu.CompilerParams(vmem_limit_bytes=SMALL)
    prepared = prepare(
        queries,
        key_codes,
        key_scale,
        outlier_chan,
        outlier_val,
        value_codes,
        value_scale,
        suffix_keys,
        suffix_values,
        page_table,
        suffix_len,
    )
    partial = attend(own, all_queries, *prepared)
    partial = lax.all_to_all(partial, near, 0, 0)
    partial = pl.pallas_call(
        merge_kernel,
        out_shape=jax.ShapeDtypeStruct((lax.axis_size(far), GROUP + STATS, LANES), BF16),
        in_specs=[VMEM],
        out_specs=VMEM,
        compiler_params=params,
        name="merge_near",
    )(partial)
    partial = lax.all_to_all(partial, far, 0, 0)
    attention = pl.pallas_call(
        merge_kernel,
        out_shape=jax.ShapeDtypeStruct((lax.axis_size(near), GROUP, LANES), BF16),
        in_specs=[VMEM],
        out_specs=VMEM,
        compiler_params=params,
        name="merge_far",
    )(partial)
    attention = lax.all_to_all(attention, near, 0, 0)
    product = pl.pallas_call(
        project_kernel,
        out_shape=jax.ShapeDtypeStruct((samples, LANES), BF16),
        in_specs=[VMEM, VMEM],
        out_specs=VMEM,
        scratch_shapes=[pltpu.VMEM((samples * HEADS, LANES), F32)],
        compiler_params=params,
        name="project",
    )(attention, out_weight)
    tp = lax.axis_size("x") * lax.axis_size("core")
    product = lax.all_to_all(product.reshape(tp, samples // tp, LANES), ("x", "core"), 0, 0)
    return pl.pallas_call(
        sum_kernel,
        out_shape=jax.ShapeDtypeStruct((samples // tp, LANES), BF16),
        in_specs=[VMEM],
        out_specs=VMEM,
        compiler_params=params,
        name="sum_tp",
    )(product)


def solution(mesh):
    grid = Mesh(mesh.devices.reshape(8, 2, 4, 4, 2), ("zh", "zl", "y", "x", "core"))
    seq, tp = ("zh", "zl", "y"), ("x", "core")
    return jax.shard_map(
        shards,
        mesh=grid,
        in_specs=(
            P(seq, tp, None),
            P(seq, tp, None),
            P(seq, tp, None),
            P(seq, tp, None),
            P(seq, tp, None),
            P(seq, tp, None),
            P(seq, tp, None),
            P(seq, None, tp, None),
            P(seq, None, tp, None),
            P(seq, None),
            P(seq),
            P(tp, seq),
        ),
        out_specs=P(tp, seq),
        check_vma=False,
    )
```

```python
import functools
import math

import jax
import jax.numpy as jnp
from jax import lax
from jax.experimental import pallas as pl
from jax.experimental.pallas import tpu as pltpu
from jax.sharding import Mesh, PartitionSpec as P

F32 = jnp.float32
BF16 = jnp.bfloat16
LANES = 128
HEADS = 8
PAGE = 128
TILE = 256
BLOCK = 2048
WEIGHT_STEP = 1024
ROOM = 256
PAGES = BLOCK // PAGE
SCORE_SCALE = math.log2(math.e) / math.sqrt(LANES)
SPLIT = 32
GROUP = 64
STATS = 8
LOW = -1e30
VMEM = pl.BlockSpec(memory_space=pltpu.VMEM)
SMEM = pl.BlockSpec(memory_space=pltpu.SMEM)
HBM = pl.BlockSpec(memory_space=pltpu.HBM)
PREPARE_LIMIT = 54 * 1024 * 1024
ATTEND_LIMIT = 53 * 1024 * 1024
SMALL = 4 * 1024 * 1024


def nt(a, b):
    return lax.dot_general(a, b, (((1,), (1,)), ((), ())), preferred_element_type=F32)


def split_rows(row):
    high = row.astype(BF16).astype(F32)
    rest = row - high
    middle = rest.astype(BF16).astype(F32)
    low = rest - middle
    part = lax.broadcasted_iota(jnp.int32, row.shape, row.ndim - 1) // SPLIT
    kept = jnp.where(part == 0, high, jnp.where(part == 1, middle, low))
    return jnp.where(part < 3, kept, 0.0).astype(BF16)


def to_lanes(columns):
    row = lax.broadcasted_iota(jnp.int32, columns.shape, 0)
    lane = lax.broadcasted_iota(jnp.int32, columns.shape, 1)
    return jnp.sum(jnp.where(lane % SPLIT == row, columns, 0.0), axis=0, keepdims=True)


def stat_rows(logs):
    copies = STATS * SPLIT // GROUP
    rows = [
        jnp.broadcast_to(to_lanes(logs[at : at + SPLIT]), (copies, LANES))
        for at in range(0, GROUP, SPLIT)
    ]
    return split_rows(jnp.concatenate(rows, axis=0))


def to_rows(stat):
    wide = jnp.broadcast_to(stat, (SPLIT, LANES))
    row = lax.broadcasted_iota(jnp.int32, wide.shape, 0)
    lane = lax.broadcasted_iota(jnp.int32, wide.shape, 1)
    return jnp.sum(jnp.where(lane % SPLIT == row, wide, 0.0), axis=1, keepdims=True)


def prepare_kernel(
    len_hbm,
    table_hbm,
    own_q_hbm,
    kscale_hbm,
    chan_hbm,
    outlier_hbm,
    vscale_hbm,
    kcodes_hbm,
    vcodes_hbm,
    skeys_hbm,
    svalues_hbm,
    keys_hbm,
    values_hbm,
    own_hbm,
    len_ref,
    table_ref,
    own_q_ref,
    kscale_ref,
    chan_ref,
    outlier_ref,
    vscale_ref,
    skbuf,
    svbuf,
    kbuf,
    vbuf,
    own_ref,
    onehot,
    ksem,
    vsem,
    kout,
    vout,
    sem,
):
    blocks = kbuf.shape[0] // BLOCK

    def block_rows(i):
        return pl.ds(pl.multiple_of(i * BLOCK, BLOCK), BLOCK)

    def chunk(hbm, buf, sems, i):
        return pltpu.make_async_copy(hbm.at[block_rows(i), :], buf.at[block_rows(i), :], sems.at[i])

    small = [
        pltpu.make_async_copy(source, target, sem.at[n])
        for n, (source, target) in enumerate(
            (
                (chan_hbm, chan_ref),
                (outlier_hbm, outlier_ref),
                (kscale_hbm, kscale_ref),
                (vscale_hbm, vscale_ref),
                (own_q_hbm, own_q_ref),
                (skeys_hbm, skbuf),
                (svalues_hbm, svbuf),
                (len_hbm, len_ref),
                (table_hbm, table_ref),
            )
        )
    ]
    result = pltpu.make_async_copy(own_ref, own_hbm.at[0], sem.at[len(small)])
    for copy in small[:3]:
        copy.start()
    for i in range(blocks):
        chunk(kcodes_hbm, kbuf, ksem, i).start()
    for copy in small[3:]:
        copy.start()
    for i in range(blocks):
        chunk(vcodes_hbm, vbuf, vsem, i).start()
    small[0].wait()

    lane = lax.broadcasted_iota(jnp.int32, (HEADS, LANES), 1)
    channels = chan_ref[...]
    for page in range(onehot.shape[0]):
        onehot[page] = (lane == channels[:, page : page + 1]).astype(F32)
    none = jnp.zeros((HEADS, LANES), F32)
    for copy in small[1:3]:
        copy.wait()

    @pl.loop(0, blocks)
    def key_block(i):
        chunk(kcodes_hbm, kbuf, ksem, i).wait()
        first_page = i * PAGES
        slots = [
            outlier_ref[:, pl.ds(pl.multiple_of((first_page + p) * PAGE, PAGE), PAGE)].astype(F32)
            for p in range(PAGES)
        ]
        slots = jnp.concatenate(slots + [none] * (LANES // HEADS - PAGES), axis=0).T.astype(BF16)
        chosen = []
        for p in range(PAGES):
            column = [none] * (LANES // HEADS)
            column[p] = onehot[first_page + p]
            chosen.append(jnp.concatenate(column, axis=0).astype(BF16))
        correction = jnp.dot(slots, jnp.concatenate(chosen, axis=1), preferred_element_type=F32)
        for p in range(PAGES):
            rows = pl.ds(pl.multiple_of((first_page + p) * PAGE, PAGE), PAGE)
            base = kbuf[rows, :].astype(F32) * kscale_ref[first_page + p]
            kbuf[rows, :] = (base + correction[:, p * LANES : (p + 1) * LANES]).astype(BF16)
        pltpu.make_async_copy(
            kbuf.at[block_rows(i), :], keys_hbm.at[block_rows(i), :], kout.at[i]
        ).start()

    for copy in small[3:]:
        copy.wait()
    live = len_ref[0]
    own_scores = [
        jnp.where(
            lane + j * PAGE < live,
            nt(own_q_ref[...], skbuf[table_ref[0, j]]) * SCORE_SCALE,
            LOW,
        )
        for j in range(skbuf.shape[0])
    ]
    top = functools.reduce(jnp.maximum, own_scores)
    top = jnp.max(top, axis=1, keepdims=True)
    sums = jnp.zeros((HEADS, LANES), F32)
    weighted = jnp.zeros((HEADS, LANES), F32)
    for j, part in enumerate(own_scores):
        weight = jnp.where(lane + j * PAGE < live, jnp.exp2(part - top), 0.0)
        sums = sums + weight
        weighted = weighted + jnp.dot(
            weight.astype(BF16), svbuf[table_ref[0, j]], preferred_element_type=F32
        )
    own_ref[0] = jnp.broadcast_to(top, (HEADS, LANES))
    own_ref[1] = jnp.broadcast_to(jnp.sum(sums, axis=1, keepdims=True), (HEADS, LANES))
    own_ref[2] = weighted
    result.start()

    @pl.loop(0, blocks)
    def value_block(i):
        chunk(vcodes_hbm, vbuf, vsem, i).wait()
        for p in range(PAGES):
            rows = pl.ds(pl.multiple_of((i * PAGES + p) * PAGE, PAGE), PAGE)
            vbuf[rows, :] = (vbuf[rows, :].astype(F32) * vscale_ref[i * PAGES + p]).astype(BF16)
        pltpu.make_async_copy(
            vbuf.at[block_rows(i), :], values_hbm.at[block_rows(i), :], vout.at[i]
        ).start()

    for i in range(blocks):
        pltpu.make_async_copy(
            kbuf.at[block_rows(i), :], keys_hbm.at[block_rows(i), :], kout.at[i]
        ).wait()
        pltpu.make_async_copy(
            vbuf.at[block_rows(i), :], values_hbm.at[block_rows(i), :], vout.at[i]
        ).wait()
    result.wait()


def attend_kernel(
    place_ref,
    q_ref,
    own_hbm,
    keys_hbm,
    values_hbm,
    out_ref,
    own_ref,
    keys_ref,
    values_ref,
    scores,
    peak,
    total,
    acc,
    ksem,
    sem,
):
    load = pltpu.make_async_copy(values_hbm, values_ref, sem.at[0])
    own_load = pltpu.make_async_copy(own_hbm.at[0], own_ref, sem.at[1])

    def chunk(i):
        rows = pl.ds(pl.multiple_of(i * BLOCK, BLOCK), BLOCK)
        return pltpu.make_async_copy(keys_hbm.at[rows, :], keys_ref.at[rows, :], ksem.at[i])

    for i in range(keys_ref.shape[0] // BLOCK):
        chunk(i).start()
    load.start()
    own_load.start()
    blocks = keys_ref.shape[0] // BLOCK
    queries = q_ref.shape[0]
    peak[...] = jnp.full(peak.shape, LOW, F32)

    @pl.loop(0, blocks)
    def score_block(i):
        chunk(i).wait()
        running = peak[...]
        for j in range(BLOCK // TILE):
            rows = pl.ds(pl.multiple_of(i * BLOCK + j * TILE, TILE), TILE)
            tile = nt(q_ref[...], keys_ref[rows, :])
            scores[i * (BLOCK // TILE) + j] = tile
            running = jnp.maximum(running, jnp.maximum(tile[:, :LANES], tile[:, LANES:]))
        peak[...] = running

    peak[...] = jnp.broadcast_to(
        jnp.max(peak[...], axis=1, keepdims=True) * SCORE_SCALE, peak.shape
    )
    total[...] = jnp.zeros(total.shape, F32)
    acc[...] = jnp.zeros(acc.shape, F32)
    load.wait()
    own_load.wait()

    @pl.loop(0, keys_ref.shape[0] // WEIGHT_STEP, unroll=True)
    def value_block(i):
        running = total[...]
        top = peak[...]
        weights = []
        for j in range(WEIGHT_STEP // TILE):
            for p in range(TILE // PAGE):
                part = scores[i * (WEIGHT_STEP // TILE) + j, :, p * LANES : (p + 1) * LANES]
                weight = jnp.exp2(part * SCORE_SCALE - top)
                running = running + weight
                weights.append(weight.astype(BF16))
        total[...] = running
        rows = pl.ds(pl.multiple_of(i * WEIGHT_STEP, WEIGHT_STEP), WEIGHT_STEP)
        acc[...] += jnp.dot(
            jnp.concatenate(weights, axis=1), values_ref[rows, :], preferred_element_type=F32
        )

    total[...] = jnp.broadcast_to(jnp.sum(total[...], axis=1, keepdims=True), total.shape)

    own = pl.ds(pl.multiple_of(place_ref[0] * HEADS, HEADS), HEADS)
    top = jnp.maximum(peak[own, :], own_ref[0])
    fade, own_fade = jnp.exp2(peak[own, :] - top), jnp.exp2(own_ref[0] - top)
    peak[own, :] = top
    total[own, :] = total[own, :] * fade + own_ref[1] * own_fade
    acc[own, :] = acc[own, :] * fade + own_ref[2] * own_fade

    pieces = out_ref.shape[0]
    for c in range(pieces):
        rows = [
            slice((u * pieces + c) * HEADS, (u * pieces + c + 1) * HEADS)
            for u in range(GROUP // HEADS)
        ]
        part = [acc[r, :] / total[r, :] for r in rows]
        logs = [peak[r, :] + jnp.log2(total[r, :]) for r in rows]
        out_ref[c, :GROUP, :] = jnp.concatenate(part, axis=0).astype(BF16)
        out_ref[c, GROUP:, :] = stat_rows(jnp.concatenate(logs, axis=0))


def merge_kernel(in_ref, out_ref):
    sources = in_ref.shape[0]
    logs = []
    for s in range(sources):
        stats = in_ref[s, GROUP:, :].astype(F32)
        first = [at * STATS // GROUP for at in range(0, GROUP, SPLIT)]
        logs.append(jnp.concatenate([to_rows(stats[at : at + 1]) for at in first], axis=0))
    top = functools.reduce(jnp.maximum, logs)
    sums = jnp.zeros(top.shape, F32)
    weighted = jnp.zeros((GROUP, LANES), F32)
    for s in range(sources):
        weight = jnp.exp2(logs[s] - top)
        sums = sums + weight
        weighted = weighted + in_ref[s, :GROUP, :].astype(F32) * weight
    merged = (weighted / sums).astype(BF16)
    copies, rows, lanes = out_ref.shape
    if rows > GROUP:
        stat = stat_rows(jnp.broadcast_to(top + jnp.log2(sums), (GROUP, LANES)))
    for c in range(copies):
        out_ref[c, :GROUP, :] = merged
        if rows > GROUP:
            out_ref[c, GROUP:, :] = stat


def project_kernel(in_ref, weight_ref, out_ref, wide):
    blocks = in_ref.shape[0]
    for c in range(blocks):
        block = in_ref[c].astype(F32)
        for u in range(GROUP // HEADS):
            first = (u * blocks + c) * HEADS
            wide[first : first + HEADS, :] = block[u * HEADS : (u + 1) * HEADS]
    samples = blocks * GROUP // HEADS
    result = jnp.zeros((samples, LANES), F32)
    for h in range(HEADS):
        part = wide[pl.ds(h, samples, stride=HEADS), :].astype(BF16)
        result = result + jnp.dot(
            part, weight_ref[h * LANES : (h + 1) * LANES, :], preferred_element_type=F32
        )
    out_ref[...] = result.astype(BF16)


def sum_kernel(in_ref, out_ref):
    result = in_ref[0].astype(F32)
    for c in range(1, in_ref.shape[0]):
        result = result + in_ref[c].astype(F32)
    out_ref[...] = result.astype(BF16)


def spread(block, axis):
    copies = jnp.broadcast_to(block[None], (lax.axis_size(axis),) + block.shape)
    return lax.all_to_all(copies, axis, 0, 0)


def prepare(
    queries,
    key_codes,
    key_scale,
    outlier_chan,
    outlier_val,
    value_codes,
    value_scale,
    suffix_keys,
    suffix_values,
    page_table,
    suffix_len,
):
    keys = key_codes.shape[0]
    pools = suffix_keys.shape[0]
    return pl.pallas_call(
        prepare_kernel,
        out_shape=(
            jax.ShapeDtypeStruct((keys, LANES), BF16),
            jax.ShapeDtypeStruct((keys, LANES), BF16),
            jax.ShapeDtypeStruct((ROOM, 3, HEADS, LANES), F32),
        ),
        in_specs=[HBM] * 11,
        out_specs=(HBM, HBM, HBM),
        scratch_shapes=[
            pltpu.SMEM(suffix_len.shape, jnp.int32),
            pltpu.SMEM(page_table.shape, jnp.int32),
            pltpu.VMEM(queries.shape, BF16),
            pltpu.VMEM(key_scale.shape, F32),
            pltpu.VMEM((HEADS, keys // PAGE), jnp.int32),
            pltpu.VMEM((HEADS, keys), BF16),
            pltpu.VMEM(value_scale.shape, F32),
            pltpu.VMEM((pools, PAGE, LANES), BF16),
            pltpu.VMEM((pools, PAGE, LANES), BF16),
            pltpu.VMEM((keys, LANES), BF16),
            pltpu.VMEM((keys, LANES), BF16),
            pltpu.VMEM((3, HEADS, LANES), F32),
            pltpu.VMEM((keys // PAGE, HEADS, LANES), F32),
            pltpu.SemaphoreType.DMA((keys // BLOCK,)),
            pltpu.SemaphoreType.DMA((keys // BLOCK,)),
            pltpu.SemaphoreType.DMA((keys // BLOCK,)),
            pltpu.SemaphoreType.DMA((keys // BLOCK,)),
            pltpu.SemaphoreType.DMA((10,)),
        ],
        compiler_params=pltpu.CompilerParams(vmem_limit_bytes=PREPARE_LIMIT),
        cost_estimate=pl.CostEstimate(
            flops=2 * keys * LANES * LANES, bytes_accessed=10 * keys * LANES, transcendentals=0
        ),
        name="prepare",
    )(
        suffix_len,
        page_table,
        queries,
        key_scale,
        outlier_chan.reshape(-1, HEADS).T,
        outlier_val.reshape(-1, HEADS).T,
        value_scale,
        key_codes.reshape(keys, LANES),
        value_codes.reshape(keys, LANES),
        suffix_keys.reshape(pools, PAGE, LANES),
        suffix_values.reshape(pools, PAGE, LANES),
    )


def attend(place, all_queries, keys, values, own):
    rows = all_queries.shape[0]
    return pl.pallas_call(
        attend_kernel,
        out_shape=jax.ShapeDtypeStruct((rows // GROUP, GROUP + STATS, LANES), BF16),
        in_specs=[SMEM, VMEM, HBM, HBM, HBM],
        out_specs=VMEM,
        scratch_shapes=[
            pltpu.VMEM(own.shape[1:], F32),
            pltpu.VMEM(keys.shape, BF16),
            pltpu.VMEM(values.shape, BF16),
            pltpu.VMEM((keys.shape[0] // TILE, rows, TILE), F32),
            pltpu.VMEM((rows, LANES), F32),
            pltpu.VMEM((rows, LANES), F32),
            pltpu.VMEM((rows, LANES), F32),
            pltpu.SemaphoreType.DMA((keys.shape[0] // BLOCK,)),
            pltpu.SemaphoreType.DMA((2,)),
        ],
        compiler_params=pltpu.CompilerParams(vmem_limit_bytes=ATTEND_LIMIT),
        name="attend",
    )(place, all_queries, own, keys, values)


def shards(
    queries,
    key_codes,
    key_scale,
    outlier_chan,
    outlier_val,
    value_codes,
    value_scale,
    suffix_keys,
    suffix_values,
    page_table,
    suffix_len,
    out_weight,
):
    seq, near, far = ("zt", "zs", "zm", "zl", "y"), ("zl", "y"), ("zm", "zs", "zt")
    samples = lax.axis_size(seq)
    queries = queries.reshape(HEADS, LANES)
    all_queries = spread(queries, seq).reshape(samples * HEADS, LANES)
    own = lax.axis_index(seq).astype(jnp.int32).reshape(1)
    params = pltpu.CompilerParams(vmem_limit_bytes=SMALL)
    prepared = prepare(
        queries,
        key_codes,
        key_scale,
        outlier_chan,
        outlier_val,
        value_codes,
        value_scale,
        suffix_keys,
        suffix_values,
        page_table,
        suffix_len,
    )
    partial = attend(own, all_queries, *prepared)
    partial = lax.all_to_all(partial, near, 0, 0)
    partial = pl.pallas_call(
        merge_kernel,
        out_shape=jax.ShapeDtypeStruct((lax.axis_size(far), GROUP + STATS, LANES), BF16),
        in_specs=[VMEM],
        out_specs=VMEM,
        compiler_params=params,
        name="merge_near",
    )(partial)
    partial = lax.all_to_all(partial, far, 0, 0)
    attention = pl.pallas_call(
        merge_kernel,
        out_shape=jax.ShapeDtypeStruct((lax.axis_size(near), GROUP, LANES), BF16),
        in_specs=[VMEM],
        out_specs=VMEM,
        compiler_params=params,
        name="merge_far",
    )(partial)
    attention = lax.all_to_all(attention, near, 0, 0)
    product = pl.pallas_call(
        project_kernel,
        out_shape=jax.ShapeDtypeStruct((samples, LANES), BF16),
        in_specs=[VMEM, VMEM],
        out_specs=VMEM,
        scratch_shapes=[pltpu.VMEM((samples * HEADS, LANES), F32)],
        compiler_params=params,
        name="project",
    )(attention, out_weight)
    tp = lax.axis_size("x") * lax.axis_size("core")
    product = lax.all_to_all(product.reshape(tp, samples // tp, LANES), ("x", "core"), 0, 0)
    return pl.pallas_call(
        sum_kernel,
        out_shape=jax.ShapeDtypeStruct((samples // tp, LANES), BF16),
        in_specs=[VMEM],
        out_specs=VMEM,
        compiler_params=params,
        name="sum_tp",
    )(product)


def solution(mesh):
    grid = Mesh(mesh.devices.reshape(2, 2, 2, 2, 4, 4, 2), ("zt", "zs", "zm", "zl", "y", "x", "core"))
    seq, tp = ("zt", "zs", "zm", "zl", "y"), ("x", "core")
    return jax.shard_map(
        shards,
        mesh=grid,
        in_specs=(
            P(seq, tp, None),
            P(seq, tp, None),
            P(seq, tp, None),
            P(seq, tp, None),
            P(seq, tp, None),
            P(seq, tp, None),
            P(seq, tp, None),
            P(seq, None, tp, None),
            P(seq, None, tp, None),
            P(seq, None),
            P(seq),
            P(tp, seq),
        ),
        out_specs=P(tp, seq),
        check_vma=False,
    )
```

```python
import functools
import math

import jax
import jax.numpy as jnp
from jax import lax
from jax.experimental import pallas as pl
from jax.experimental.pallas import tpu as pltpu
from jax.sharding import Mesh, PartitionSpec as P

F32 = jnp.float32
BF16 = jnp.bfloat16
LANES = 128
HEADS = 8
PAGE = 128
TILE = 256
BLOCK = 2048
WEIGHT_STEP = 1024
WIDTH = 4
ROOM = 256
PAGES = BLOCK // PAGE
SCORE_SCALE = math.log2(math.e) / math.sqrt(LANES)
SPLIT = 32
GROUP = 64
STATS = 8
LOW = -1e30
VMEM = pl.BlockSpec(memory_space=pltpu.VMEM)
SMEM = pl.BlockSpec(memory_space=pltpu.SMEM)
HBM = pl.BlockSpec(memory_space=pltpu.HBM)
PREPARE_LIMIT = 54 * 1024 * 1024
ATTEND_LIMIT = 53 * 1024 * 1024
SMALL = 4 * 1024 * 1024


def nt(a, b):
    return lax.dot_general(a, b, (((1,), (1,)), ((), ())), preferred_element_type=F32)


def split_rows(row):
    high = row.astype(BF16).astype(F32)
    rest = row - high
    middle = rest.astype(BF16).astype(F32)
    low = rest - middle
    part = lax.broadcasted_iota(jnp.int32, row.shape, row.ndim - 1) // SPLIT
    kept = jnp.where(part == 0, high, jnp.where(part == 1, middle, low))
    return jnp.where(part < 3, kept, 0.0).astype(BF16)


def to_lanes(columns):
    row = lax.broadcasted_iota(jnp.int32, columns.shape, 0)
    lane = lax.broadcasted_iota(jnp.int32, columns.shape, 1)
    return jnp.sum(jnp.where(lane % SPLIT == row, columns, 0.0), axis=0, keepdims=True)


def stat_rows(logs):
    copies = STATS * SPLIT // GROUP
    rows = [
        jnp.broadcast_to(to_lanes(logs[at : at + SPLIT]), (copies, LANES))
        for at in range(0, GROUP, SPLIT)
    ]
    return split_rows(jnp.concatenate(rows, axis=0))


def to_rows(stat):
    wide = jnp.broadcast_to(stat, (SPLIT, LANES))
    row = lax.broadcasted_iota(jnp.int32, wide.shape, 0)
    lane = lax.broadcasted_iota(jnp.int32, wide.shape, 1)
    return jnp.sum(jnp.where(lane % SPLIT == row, wide, 0.0), axis=1, keepdims=True)


def place_of(c, u, pieces, depth):
    low, y = c // WIDTH, c % WIDTH
    pairs = pieces // WIDTH
    return (y * depth + u) * pairs + low


def prepare_kernel(
    len_hbm,
    table_hbm,
    own_q_hbm,
    kscale_hbm,
    chan_hbm,
    outlier_hbm,
    vscale_hbm,
    kcodes_hbm,
    vcodes_hbm,
    skeys_hbm,
    svalues_hbm,
    keys_hbm,
    values_hbm,
    own_hbm,
    len_ref,
    table_ref,
    own_q_ref,
    kscale_ref,
    chan_ref,
    outlier_ref,
    vscale_ref,
    skbuf,
    svbuf,
    kbuf,
    vbuf,
    own_ref,
    onehot,
    ksem,
    vsem,
    kout,
    vout,
    sem,
):
    blocks = kbuf.shape[0] // BLOCK

    def block_rows(i):
        return pl.ds(pl.multiple_of(i * BLOCK, BLOCK), BLOCK)

    def chunk(hbm, buf, sems, i):
        return pltpu.make_async_copy(hbm.at[block_rows(i), :], buf.at[block_rows(i), :], sems.at[i])

    small = [
        pltpu.make_async_copy(source, target, sem.at[n])
        for n, (source, target) in enumerate(
            (
                (chan_hbm, chan_ref),
                (outlier_hbm, outlier_ref),
                (kscale_hbm, kscale_ref),
                (vscale_hbm, vscale_ref),
                (own_q_hbm, own_q_ref),
                (skeys_hbm, skbuf),
                (svalues_hbm, svbuf),
                (len_hbm, len_ref),
                (table_hbm, table_ref),
            )
        )
    ]
    result = pltpu.make_async_copy(own_ref, own_hbm.at[0], sem.at[len(small)])
    for copy in small[:3]:
        copy.start()
    for i in range(blocks):
        chunk(kcodes_hbm, kbuf, ksem, i).start()
    for copy in small[3:]:
        copy.start()
    for i in range(blocks):
        chunk(vcodes_hbm, vbuf, vsem, i).start()
    small[0].wait()

    lane = lax.broadcasted_iota(jnp.int32, (HEADS, LANES), 1)
    channels = chan_ref[...]
    for page in range(onehot.shape[0]):
        onehot[page] = (lane == channels[:, page : page + 1]).astype(F32)
    none = jnp.zeros((HEADS, LANES), F32)
    for copy in small[1:3]:
        copy.wait()

    @pl.loop(0, blocks)
    def key_block(i):
        chunk(kcodes_hbm, kbuf, ksem, i).wait()
        first_page = i * PAGES
        slots = [
            outlier_ref[:, pl.ds(pl.multiple_of((first_page + p) * PAGE, PAGE), PAGE)].astype(F32)
            for p in range(PAGES)
        ]
        slots = jnp.concatenate(slots + [none] * (LANES // HEADS - PAGES), axis=0).T.astype(BF16)
        chosen = []
        for p in range(PAGES):
            column = [none] * (LANES // HEADS)
            column[p] = onehot[first_page + p]
            chosen.append(jnp.concatenate(column, axis=0).astype(BF16))
        correction = jnp.dot(slots, jnp.concatenate(chosen, axis=1), preferred_element_type=F32)
        for p in range(PAGES):
            rows = pl.ds(pl.multiple_of((first_page + p) * PAGE, PAGE), PAGE)
            base = kbuf[rows, :].astype(F32) * kscale_ref[first_page + p]
            kbuf[rows, :] = (base + correction[:, p * LANES : (p + 1) * LANES]).astype(BF16)
        pltpu.make_async_copy(
            kbuf.at[block_rows(i), :], keys_hbm.at[block_rows(i), :], kout.at[i]
        ).start()

    for copy in small[3:]:
        copy.wait()
    live = len_ref[0]
    own_scores = [
        jnp.where(
            lane + j * PAGE < live,
            nt(own_q_ref[...], skbuf[table_ref[0, j]]) * SCORE_SCALE,
            LOW,
        )
        for j in range(skbuf.shape[0])
    ]
    top = functools.reduce(jnp.maximum, own_scores)
    top = jnp.max(top, axis=1, keepdims=True)
    sums = jnp.zeros((HEADS, LANES), F32)
    weighted = jnp.zeros((HEADS, LANES), F32)
    for j, part in enumerate(own_scores):
        weight = jnp.where(lane + j * PAGE < live, jnp.exp2(part - top), 0.0)
        sums = sums + weight
        weighted = weighted + jnp.dot(
            weight.astype(BF16), svbuf[table_ref[0, j]], preferred_element_type=F32
        )
    own_ref[0] = jnp.broadcast_to(top, (HEADS, LANES))
    own_ref[1] = jnp.broadcast_to(jnp.sum(sums, axis=1, keepdims=True), (HEADS, LANES))
    own_ref[2] = weighted
    result.start()

    @pl.loop(0, blocks)
    def value_block(i):
        chunk(vcodes_hbm, vbuf, vsem, i).wait()
        for p in range(PAGES):
            rows = pl.ds(pl.multiple_of((i * PAGES + p) * PAGE, PAGE), PAGE)
            vbuf[rows, :] = (vbuf[rows, :].astype(F32) * vscale_ref[i * PAGES + p]).astype(BF16)
        pltpu.make_async_copy(
            vbuf.at[block_rows(i), :], values_hbm.at[block_rows(i), :], vout.at[i]
        ).start()

    for i in range(blocks):
        pltpu.make_async_copy(
            kbuf.at[block_rows(i), :], keys_hbm.at[block_rows(i), :], kout.at[i]
        ).wait()
        pltpu.make_async_copy(
            vbuf.at[block_rows(i), :], values_hbm.at[block_rows(i), :], vout.at[i]
        ).wait()
    result.wait()


def attend_kernel(
    place_ref,
    q_ref,
    own_hbm,
    keys_hbm,
    values_hbm,
    out_ref,
    own_ref,
    keys_ref,
    values_ref,
    scores,
    peak,
    total,
    acc,
    ksem,
    sem,
):
    load = pltpu.make_async_copy(values_hbm, values_ref, sem.at[0])
    own_load = pltpu.make_async_copy(own_hbm.at[0], own_ref, sem.at[1])

    def chunk(i):
        rows = pl.ds(pl.multiple_of(i * BLOCK, BLOCK), BLOCK)
        return pltpu.make_async_copy(keys_hbm.at[rows, :], keys_ref.at[rows, :], ksem.at[i])

    for i in range(keys_ref.shape[0] // BLOCK):
        chunk(i).start()
    load.start()
    own_load.start()
    blocks = keys_ref.shape[0] // BLOCK
    queries = q_ref.shape[0]
    peak[...] = jnp.full(peak.shape, LOW, F32)

    @pl.loop(0, blocks)
    def score_block(i):
        chunk(i).wait()
        running = peak[...]
        for j in range(BLOCK // TILE):
            rows = pl.ds(pl.multiple_of(i * BLOCK + j * TILE, TILE), TILE)
            tile = nt(q_ref[...], keys_ref[rows, :])
            scores[i * (BLOCK // TILE) + j] = tile
            running = jnp.maximum(running, jnp.maximum(tile[:, :LANES], tile[:, LANES:]))
        peak[...] = running

    peak[...] = jnp.broadcast_to(
        jnp.max(peak[...], axis=1, keepdims=True) * SCORE_SCALE, peak.shape
    )
    total[...] = jnp.zeros(total.shape, F32)
    acc[...] = jnp.zeros(acc.shape, F32)
    load.wait()
    own_load.wait()

    @pl.loop(0, keys_ref.shape[0] // WEIGHT_STEP, unroll=True)
    def value_block(i):
        running = total[...]
        top = peak[...]
        weights = []
        for j in range(WEIGHT_STEP // TILE):
            for p in range(TILE // PAGE):
                part = scores[i * (WEIGHT_STEP // TILE) + j, :, p * LANES : (p + 1) * LANES]
                weight = jnp.exp2(part * SCORE_SCALE - top)
                running = running + weight
                weights.append(weight.astype(BF16))
        total[...] = running
        rows = pl.ds(pl.multiple_of(i * WEIGHT_STEP, WEIGHT_STEP), WEIGHT_STEP)
        acc[...] += jnp.dot(
            jnp.concatenate(weights, axis=1), values_ref[rows, :], preferred_element_type=F32
        )

    total[...] = jnp.broadcast_to(jnp.sum(total[...], axis=1, keepdims=True), total.shape)

    own = pl.ds(pl.multiple_of(place_ref[0] * HEADS, HEADS), HEADS)
    top = jnp.maximum(peak[own, :], own_ref[0])
    fade, own_fade = jnp.exp2(peak[own, :] - top), jnp.exp2(own_ref[0] - top)
    peak[own, :] = top
    total[own, :] = total[own, :] * fade + own_ref[1] * own_fade
    acc[own, :] = acc[own, :] * fade + own_ref[2] * own_fade

    pieces = out_ref.shape[0]
    for c in range(pieces):
        rows = [
            slice(at * HEADS, (at + 1) * HEADS)
            for at in (place_of(c, u, pieces, GROUP // HEADS) for u in range(GROUP // HEADS))
        ]
        part = [acc[r, :] / total[r, :] for r in rows]
        logs = [peak[r, :] + jnp.log2(total[r, :]) for r in rows]
        out_ref[c, :GROUP, :] = jnp.concatenate(part, axis=0).astype(BF16)
        out_ref[c, GROUP:, :] = stat_rows(jnp.concatenate(logs, axis=0))


def merge_kernel(in_ref, out_ref):
    sources = in_ref.shape[0]
    logs = []
    for s in range(sources):
        stats = in_ref[s, GROUP:, :].astype(F32)
        first = [at * STATS // GROUP for at in range(0, GROUP, SPLIT)]
        logs.append(jnp.concatenate([to_rows(stats[at : at + 1]) for at in first], axis=0))
    top = functools.reduce(jnp.maximum, logs)
    sums = jnp.zeros(top.shape, F32)
    weighted = jnp.zeros((GROUP, LANES), F32)
    for s in range(sources):
        weight = jnp.exp2(logs[s] - top)
        sums = sums + weight
        weighted = weighted + in_ref[s, :GROUP, :].astype(F32) * weight
    merged = (weighted / sums).astype(BF16)
    copies, rows, lanes = out_ref.shape
    if rows > GROUP:
        stat = stat_rows(jnp.broadcast_to(top + jnp.log2(sums), (GROUP, LANES)))
    for c in range(copies):
        out_ref[c, :GROUP, :] = merged
        if rows > GROUP:
            out_ref[c, GROUP:, :] = stat


def project_kernel(in_ref, weight_ref, out_ref, wide):
    blocks = in_ref.shape[0]
    for c in range(blocks):
        block = in_ref[c].astype(F32)
        for u in range(GROUP // HEADS):
            first = (u * blocks + c) * HEADS
            wide[first : first + HEADS, :] = block[u * HEADS : (u + 1) * HEADS]
    samples = blocks * GROUP // HEADS
    result = jnp.zeros((samples, LANES), F32)
    for h in range(HEADS):
        part = wide[pl.ds(h, samples, stride=HEADS), :].astype(BF16)
        result = result + jnp.dot(
            part, weight_ref[h * LANES : (h + 1) * LANES, :], preferred_element_type=F32
        )
    out_ref[...] = result.astype(BF16)


def sum_kernel(in_ref, out_ref):
    result = in_ref[0].astype(F32)
    for c in range(1, in_ref.shape[0]):
        result = result + in_ref[c].astype(F32)
    out_ref[...] = result.astype(BF16)


def spread(block, axis):
    copies = jnp.broadcast_to(block[None], (lax.axis_size(axis),) + block.shape)
    return lax.all_to_all(copies, axis, 0, 0)


def prepare(
    queries,
    key_codes,
    key_scale,
    outlier_chan,
    outlier_val,
    value_codes,
    value_scale,
    suffix_keys,
    suffix_values,
    page_table,
    suffix_len,
):
    keys = key_codes.shape[0]
    pools = suffix_keys.shape[0]
    return pl.pallas_call(
        prepare_kernel,
        out_shape=(
            jax.ShapeDtypeStruct((keys, LANES), BF16),
            jax.ShapeDtypeStruct((keys, LANES), BF16),
            jax.ShapeDtypeStruct((ROOM, 3, HEADS, LANES), F32),
        ),
        in_specs=[HBM] * 11,
        out_specs=(HBM, HBM, HBM),
        scratch_shapes=[
            pltpu.SMEM(suffix_len.shape, jnp.int32),
            pltpu.SMEM(page_table.shape, jnp.int32),
            pltpu.VMEM(queries.shape, BF16),
            pltpu.VMEM(key_scale.shape, F32),
            pltpu.VMEM((HEADS, keys // PAGE), jnp.int32),
            pltpu.VMEM((HEADS, keys), BF16),
            pltpu.VMEM(value_scale.shape, F32),
            pltpu.VMEM((pools, PAGE, LANES), BF16),
            pltpu.VMEM((pools, PAGE, LANES), BF16),
            pltpu.VMEM((keys, LANES), BF16),
            pltpu.VMEM((keys, LANES), BF16),
            pltpu.VMEM((3, HEADS, LANES), F32),
            pltpu.VMEM((keys // PAGE, HEADS, LANES), F32),
            pltpu.SemaphoreType.DMA((keys // BLOCK,)),
            pltpu.SemaphoreType.DMA((keys // BLOCK,)),
            pltpu.SemaphoreType.DMA((keys // BLOCK,)),
            pltpu.SemaphoreType.DMA((keys // BLOCK,)),
            pltpu.SemaphoreType.DMA((10,)),
        ],
        compiler_params=pltpu.CompilerParams(vmem_limit_bytes=PREPARE_LIMIT),
        cost_estimate=pl.CostEstimate(
            flops=2 * keys * LANES * LANES, bytes_accessed=10 * keys * LANES, transcendentals=0
        ),
        name="prepare",
    )(
        suffix_len,
        page_table,
        queries,
        key_scale,
        outlier_chan.reshape(-1, HEADS).T,
        outlier_val.reshape(-1, HEADS).T,
        value_scale,
        key_codes.reshape(keys, LANES),
        value_codes.reshape(keys, LANES),
        suffix_keys.reshape(pools, PAGE, LANES),
        suffix_values.reshape(pools, PAGE, LANES),
    )


def attend(place, all_queries, keys, values, own):
    rows = all_queries.shape[0]
    return pl.pallas_call(
        attend_kernel,
        out_shape=jax.ShapeDtypeStruct((rows // GROUP, GROUP + STATS, LANES), BF16),
        in_specs=[SMEM, VMEM, HBM, HBM, HBM],
        out_specs=VMEM,
        scratch_shapes=[
            pltpu.VMEM(own.shape[1:], F32),
            pltpu.VMEM(keys.shape, BF16),
            pltpu.VMEM(values.shape, BF16),
            pltpu.VMEM((keys.shape[0] // TILE, rows, TILE), F32),
            pltpu.VMEM((rows, LANES), F32),
            pltpu.VMEM((rows, LANES), F32),
            pltpu.VMEM((rows, LANES), F32),
            pltpu.SemaphoreType.DMA((keys.shape[0] // BLOCK,)),
            pltpu.SemaphoreType.DMA((2,)),
        ],
        compiler_params=pltpu.CompilerParams(vmem_limit_bytes=ATTEND_LIMIT),
        name="attend",
    )(place, all_queries, own, keys, values)


def shards(
    queries,
    key_codes,
    key_scale,
    outlier_chan,
    outlier_val,
    value_codes,
    value_scale,
    suffix_keys,
    suffix_values,
    page_table,
    suffix_len,
    out_weight,
):
    seq, near, far = ("zt", "zs", "zm", "zl", "y"), ("zl", "y"), ("zm", "zs", "zt")
    gather = ("y", "zt", "zs", "zm", "zl")
    samples = lax.axis_size(seq)
    queries = queries.reshape(HEADS, LANES)
    all_queries = spread(queries, gather).reshape(samples * HEADS, LANES)
    own = lax.axis_index(gather).astype(jnp.int32).reshape(1)
    params = pltpu.CompilerParams(vmem_limit_bytes=SMALL)
    prepared = prepare(
        queries,
        key_codes,
        key_scale,
        outlier_chan,
        outlier_val,
        value_codes,
        value_scale,
        suffix_keys,
        suffix_values,
        page_table,
        suffix_len,
    )
    partial = attend(own, all_queries, *prepared)
    partial = lax.all_to_all(partial, near, 0, 0)
    partial = pl.pallas_call(
        merge_kernel,
        out_shape=jax.ShapeDtypeStruct((lax.axis_size(far), GROUP + STATS, LANES), BF16),
        in_specs=[VMEM],
        out_specs=VMEM,
        compiler_params=params,
        name="merge_near",
    )(partial)
    partial = lax.all_to_all(partial, far, 0, 0)
    attention = pl.pallas_call(
        merge_kernel,
        out_shape=jax.ShapeDtypeStruct((lax.axis_size(near), GROUP, LANES), BF16),
        in_specs=[VMEM],
        out_specs=VMEM,
        compiler_params=params,
        name="merge_far",
    )(partial)
    attention = lax.all_to_all(attention, near, 0, 0)
    product = pl.pallas_call(
        project_kernel,
        out_shape=jax.ShapeDtypeStruct((samples, LANES), BF16),
        in_specs=[VMEM, VMEM],
        out_specs=VMEM,
        scratch_shapes=[pltpu.VMEM((samples * HEADS, LANES), F32)],
        compiler_params=params,
        name="project",
    )(attention, out_weight)
    tp = lax.axis_size("x") * lax.axis_size("core")
    product = lax.all_to_all(product.reshape(tp, samples // tp, LANES), ("x", "core"), 0, 0)
    return pl.pallas_call(
        sum_kernel,
        out_shape=jax.ShapeDtypeStruct((samples // tp, LANES), BF16),
        in_specs=[VMEM],
        out_specs=VMEM,
        compiler_params=params,
        name="sum_tp",
    )(product)


def solution(mesh):
    grid = Mesh(mesh.devices.reshape(2, 2, 2, 2, 4, 4, 2), ("zt", "zs", "zm", "zl", "y", "x", "core"))
    seq, tp = ("zt", "zs", "zm", "zl", "y"), ("x", "core")
    return jax.shard_map(
        shards,
        mesh=grid,
        in_specs=(
            P(seq, tp, None),
            P(seq, tp, None),
            P(seq, tp, None),
            P(seq, tp, None),
            P(seq, tp, None),
            P(seq, tp, None),
            P(seq, tp, None),
            P(seq, None, tp, None),
            P(seq, None, tp, None),
            P(seq, None),
            P(seq),
            P(tp, seq),
        ),
        out_specs=P(tp, seq),
        check_vma=False,
    )
```
